512 devices in a mesh: pix: 32 (over z_hi, x, core), mz: 16 (over y, z_lo).
Axes of the slice: x: 4, y: 8, z: 8 (z_hi: 4, z_lo: 2; z = z_hi * 2 + z_lo), core: 2. Of those that a mesh axis runs over, the one named last changes fastest.
Arguments:
- spectra: bfloat16 [128, 256, 2048], P('pix', None, 'mz'), may hold values from -6 to 6
- scores: float32 [128, 16384], P('pix'), may hold values from -6 to 6
- loadings: float32 [2048, 64], P('mz'), may hold values from -0.75 to 0.75
- smooth: float32 [64], replicated, may hold values from 0.3 to 3
- thresholds: float32 [2048], P('mz'), may hold values from 0.1 to 1.5
- across: int32 [128, 256], P('pix'), may hold values from 0 to 3
- down: int32 [128, 256], P('pix'), may hold values from 0 to 3
Outputs:
- score_maps: float32 [128, 16384], P('pix')
- final_loadings: float32 [2048, 64], P('mz')
- sparse_part: bfloat16 [128, 256, 2048], P('pix', None, 'mz')
The draws below stay inside these ranges and needn't reach their ends.
All inputs are finite; a program needn't handle non-finite values.
Results may differ from the reference program's by a relative error of at most 0.001.
Values sent between devices are 32-bit elements; how exact they have to be, the bound alone decides.
A program may use at most 64 MiB of HBM per device.

```python
import math
import jax
import jax.numpy as jnp
from jax import lax

IMG_COLS = 256
BINS = 2048
RANK = 64
ITERS = 3
IMG_ROWS = 128


def touch_ends(entries, stream_key, smallest, high):
    shape = entries.shape
    place = [jax.random.randint(jax.random.fold_in(stream_key, axis), (), 0, shape[axis]) for axis in range(len(shape))]
    entries = entries.at[tuple(place)].set(smallest)
    longest = shape.index(max(shape))
    place[longest] = (place[longest] + 1) % shape[longest]
    return entries.at[tuple(place)].set(high)


def block_levels(stream_key, shape, cuts, low, largest):
    def one(axis_at, blocks):
        steps = jax.random.uniform(jax.random.fold_in(jax.random.fold_in(stream_key, 6), axis_at), (blocks,), jnp.float32, low / len(cuts), largest / len(cuts))
        return jnp.repeat(jnp.exp(steps), shape[axis_at] // blocks).reshape((-1,) + (1,) * (len(shape) - axis_at - 1))

    loudness = one(*cuts[0])
    for cut in cuts[1:]:
        loudness = loudness * one(*cut)
    return loudness


def scatter_about(own_key, dims, deviation, reach, cuts=(), dtype=jnp.bfloat16):
    drawn = jax.random.normal(own_key, dims, jnp.float32) * deviation
    if len(cuts) > 0:
        drawn = block_levels(own_key, dims, cuts, -0.22, 0.18) * drawn
    return jnp.clip(drawn, min=-reach, max=reach).astype(dtype)


def setup_inputs(seed: int = 0) -> dict:
    key_of = jax.random.split(jax.random.key(seed), 8)
    return {
        "spectra": scatter_about(key_of[0], (IMG_ROWS, IMG_COLS, BINS), 1.0, 6.0, ((0, 32), (2, 16))),
        "scores": scatter_about(key_of[1], (IMG_ROWS, IMG_COLS * RANK), 1.0, 6.0, ((0, 32),), jnp.float32),
        "loadings": scatter_about(key_of[2], (BINS, RANK), RANK ** -0.5, 0.75, ((0, 16),), jnp.float32),
        "smooth": jnp.clip(jnp.exp(jax.random.uniform(key_of[3], (RANK,), jnp.float32, math.log(0.3), math.log(3.0))), 0.3, 3.0),
        "thresholds": jnp.clip(jnp.exp(math.log(1.5) - 2.7080502 * jax.random.uniform(key_of[4], (BINS,), jnp.float32) ** block_levels(key_of[4], (BINS,), ((0, 16),), -0.2, 0.2)), 0.1, 1.5),
        "across": touch_ends(jax.random.randint(key_of[5], (IMG_ROWS, IMG_COLS), 0, 4), jax.random.fold_in(key_of[5], 1), 0, 3).astype(jnp.int32),
        "down": touch_ends(jax.random.randint(key_of[6], (IMG_ROWS, IMG_COLS), 0, 4), jax.random.fold_in(key_of[6], 1), 0, 3).astype(jnp.int32),
    }


def laplace(u3, w_right, w_down, smooth):
    zero_row = jnp.zeros_like(u3[:1])
    nxt = jnp.concatenate([u3[1:], zero_row], axis=0)
    flow_v = w_down[:, :, None] * (u3 - nxt)
    lap_v = flow_v - jnp.concatenate([jnp.zeros_like(flow_v[:1]), flow_v[:-1]], axis=0)
    zero_col = jnp.zeros_like(u3[:, :1])
    right = jnp.concatenate([u3[:, 1:], zero_col], axis=1)
    flow_h = w_right[:, :, None] * (u3 - right)
    lap_h = flow_h - jnp.concatenate([jnp.zeros_like(flow_h[:, :1]), flow_h[:, :-1]], axis=1)
    return (lap_v + lap_h) * smooth[None, None, :]


def reference(spectra, scores, loadings, smooth, thresholds, across, down):
    hi = lax.Precision.HIGHEST
    nrows, ncols, nbins = spectra.shape
    rank = loadings.shape[1]
    data = spectra.astype(jnp.float32).reshape(nrows * ncols, nbins)
    row_idx = jnp.arange(nrows)[:, None]
    col_idx = jnp.arange(ncols)[None, :]
    w_right = jnp.where(col_idx < ncols - 1, (across.astype(jnp.float32) + 1.0) * 0.25, 0.0)
    w_down = jnp.where(row_idx < nrows - 1, (down.astype(jnp.float32) + 1.0) * 0.25, 0.0)
    u = scores.reshape(nrows * ncols, rank)
    v = loadings
    approx = jnp.dot(u, v.T, precision=hi, preferred_element_type=jnp.float32)
    sparse = jnp.zeros_like(data)
    dual = jnp.zeros_like(data)
    for step in range(ITERS):
        resid = approx + sparse - data + dual
        grad = jnp.dot(resid, v, precision=hi, preferred_element_type=jnp.float32)
        vgrad = jnp.dot(resid.T, u, precision=hi, preferred_element_type=jnp.float32)
        usq = jnp.sum(u * u)
        vsq = jnp.sum(v * v)
        eta_u = 1.0 / (vsq / rank + 8.0 * smooth + 1.0)
        eta_v = 1.0 / (usq / rank + 1.0)
        lap = laplace(u.reshape(nrows, ncols, rank), w_right, w_down, smooth).reshape(nrows * ncols, rank)
        u = u - eta_u[None, :] * (grad + lap)
        v = v - eta_v * vgrad
        approx = jnp.dot(u, v.T, precision=hi, preferred_element_type=jnp.float32)
        target = data - approx - dual
        sparse = target - jnp.clip(target, -thresholds[None, :], thresholds[None, :])
        dual = dual + approx + sparse - data
    return (u.reshape(nrows, ncols * rank), v,
            sparse.reshape(nrows, ncols, nbins).astype(jnp.bfloat16))
```

```python
import functools
import jax
import jax.numpy as jnp
from jax import lax
from jax.experimental import pallas as pl
from jax.experimental.pallas import tpu as pltpu
from jax.sharding import PartitionSpec as P

ITERS = 3
GROUP = 8
MESH = pl.DeviceIdType.MESH
F32 = jnp.float32
BF16 = jnp.bfloat16
NT = (((1,), (1,)), ((), ()))
TN = (((0,), (0,)), ((), ()))


def mm(a, b, dims=(((1,), (0,)), ((), ()))):
    return lax.dot_general(a, b, dims, preferred_element_type=F32)


def split(a):
    high = a.astype(BF16)
    return high, (a - high.astype(F32)).astype(BF16)


def kernel(
    group,
    x_hbm, u_hbm, v_hbm, smooth_hbm, thr_hbm, across_hbm, down_hbm,
    uo_hbm, vo_hbm, so_hbm,
    x_in, u_in, v_in, smooth_in, thr_in, across_in, down_in, down_above,
    xf, x_e, x_o, c_e, c_o, u_hl, d_h, d_l, b_hh, b_hl, ubuf, vbuf,
    g_send, g_recv, h_send, h_recv, z_recv, halo_send, halo_recv,
    wtmp, shift, weights,
    in_sems, out_sems, g_ssem, g_rsem, u_ssem, u_rsem, h_ssem, h_rsem, z_ssem, z_rsem,
    v_ssem, v_rsem, halo_ssem, halo_rsem, down_ssem, down_rsem,
):
    n_pix, n_mz = lax.axis_size("pix"), lax.axis_size("mz")
    pix, mz = lax.axis_index("pix"), lax.axis_index("mz")
    n_z = n_pix // group
    zed, spot = pix // group, pix % group
    rows, cols, bins = x_in.shape
    rank = v_in.shape[1]
    nq = rows * cols // 2
    piece = nq // n_mz
    pairs = piece // rows
    srows = rank // group
    below, above = (pix + 1) % n_pix, (pix + n_pix - 1) % n_pix

    barrier = pltpu.get_barrier_semaphore()

    def greet(device):
        pl.semaphore_signal(barrier, inc=1, device_id=device, device_id_type=MESH)

    def each(count, act):
        lax.fori_loop(1, count, lambda i, _: (act(i), 0)[1], 0)

    def mz_peer(i):
        return (mz + i) % n_mz

    def group_peer(i):
        return (spot + i) % group

    def z_peer(i):
        return (zed + i) % n_z

    each(n_mz, lambda i: greet((pix, mz_peer(i))))
    each(group, lambda i: greet((zed * group + group_peer(i), mz)))
    each(n_z, lambda i: greet((z_peer(i) * group + spot, mz)))
    greet((below, mz))
    greet((above, mz))

    loads = [
        pltpu.make_async_copy(src, dst, in_sems.at[i])
        for i, (src, dst) in enumerate(
            [
                (u_hbm, u_in), (v_hbm, v_in), (x_hbm, x_in), (down_hbm, down_in),
                (across_hbm, across_in), (smooth_hbm, smooth_in), (thr_hbm, thr_in),
            ]
        )
    ]
    for load in loads:
        load.start()

    def remote(src, dst, ssem, rsem, device):
        return pltpu.make_async_remote_copy(
            src_ref=src, dst_ref=dst, send_sem=ssem, recv_sem=rsem,
            device_id=device, device_id_type=MESH,
        )

    def drain(ref, sem):
        pltpu.make_async_copy(ref, ref, sem).wait()

    def my_rows(base=8):
        return pl.ds(pl.multiple_of(base + piece * mz, 8), piece)

    loads[0].wait()
    zeros8 = jnp.zeros((8, 128), F32)
    for k in range(ITERS + 1):
        ubuf[k, 0:8, :] = zeros8
        ubuf[k, 8 + nq : 16 + nq, :] = zeros8
    for t in range(cols // 2):
        ubuf[0, 8 + rows * t : 8 + rows * (t + 1), :] = u_in[:, 128 * t : 128 * (t + 1)]

    pl.semaphore_wait(barrier, n_mz - 1 + group - 1 + n_z - 1 + 2)

    def halos(k):
        up = remote(
            halo_send.at[k, 0], halo_recv.at[k, 1], halo_ssem.at[k, 0], halo_rsem.at[k, 1],
            (above, mz),
        )
        down = remote(
            halo_send.at[k, 1], halo_recv.at[k, 0], halo_ssem.at[k, 1], halo_rsem.at[k, 0],
            (below, mz),
        )
        return up, down

    def send_halos(k, mine):
        shift[0] = mine
        halo_send[k, 0] = shift[0, pl.ds(0, pairs, stride=rows), :]
        halo_send[k, 1] = shift[0, pl.ds(rows - 1, pairs, stride=rows), :]
        for copy in halos(k):
            copy.start()

    send_halos(0, ubuf[0, my_rows(), :])
    loads[3].wait()
    down_copy = remote(down_in, down_above, down_ssem, down_rsem, (below, mz))
    down_copy.start()

    loads[1].wait()
    vbuf[0] = v_in[...].T
    loads[2].wait()
    xf[...] = x_in[...].reshape(rows * cols, bins).astype(F32)
    for r in range(rows):
        for par, dst in ((0, x_e), (1, x_o)):
            dst[pl.ds(r, cols // 2, stride=rows), :] = xf[
                pl.ds(r * cols + par, cols // 2, stride=2), :
            ]
    for load in loads[4:]:
        load.wait()
    thr = thr_in[...]

    b_hh[...] = jnp.zeros_like(b_hh)
    b_hl[...] = jnp.zeros_like(b_hl)
    chunk = max(128, piece)

    def factors(k):
        high, low = split(vbuf[k])
        for at, part in ((0, high), (128, high)):
            b_hh[at : at + rank, 0:bins] = part
            b_hh[at + rank : at + 2 * rank, bins : 2 * bins] = part
        for at, part in ((0, high), (128, low)):
            b_hl[at : at + rank, 0:bins] = part
            b_hl[at + rank : at + 2 * rank, bins : 2 * bins] = part

    def send_g(k, j):
        return remote(
            g_send.at[k, j], g_recv.at[k, mz], g_ssem.at[k], g_rsem.at[k], (pix, j)
        )

    def sweep(k):
        factors(k)
        usq = jnp.zeros((8, 128), F32)
        vsq = jnp.sum(vbuf[k] * vbuf[k], axis=0, keepdims=True)
        for q in range(0, nq, chunk):
            here = pl.ds(q, chunk)
            u = ubuf[k, q + 8 : q + 8 + chunk, :]
            u_h, u_l = split(u)
            u_hl[here, 0:128] = u_h
            u_hl[here, 128:256] = u_l
            usq = usq + jnp.sum((u * u).reshape(chunk // 8, 8, 128), axis=0)
            approx = mm(u_hl[here, :], b_hh[...]) + mm(u_h, b_hl[128:256, :])
            for par, x, c in ((0, x_e, c_e), (1, x_o, c_o)):
                low = approx[:, par * bins : (par + 1) * bins]
                if k == 0:
                    d = low - x[here, :]
                else:
                    t = x[here, :] - low
                    if k > 1:
                        old = c[here, :]
                        t = t + old
                    clipped = jnp.clip(t, -thr, thr)
                    if k == ITERS:
                        c[here, :] = t - clipped
                        continue
                    c[here, :] = clipped
                    d = -2.0 * clipped
                    if k > 1:
                        d = d + old
                high, low = split(d)
                d_h[here, par * bins : (par + 1) * bins] = high
                d_l[here, par * bins : (par + 1) * bins] = low
            if k == ITERS:
                continue
            g2 = mm(d_h[here, :], b_hl[...], NT)
            g = g2[:, 0:128] + g2[:, 128:256] + mm(d_l[here, :], b_hh[0:128, :], NT)
            for j in range(q // piece, (q + chunk) // piece):
                g_send[k, j, 0:piece, :] = g[j * piece - q : (j + 1) * piece - q, :]
                g_send[k, j, piece : piece + 1, :] = vsq
        return usq

    def gradients(k):
        usq = sweep(k)
        each(n_mz, lambda i: send_g(k, mz_peer(i)).start())
        both = mm(u_hl[...], d_h[...], TN)
        prod = both[0:128, :] + both[128:256, :] + mm(u_hl[:, 0:128], d_l[...], TN)
        h = prod[0:rank, 0:bins] + prod[rank : 2 * rank, bins : 2 * bins]
        for j in range(group):
            h_send[k, j, 0:srows, :] = h[j * srows : (j + 1) * srows, :]
            h_send[k, j, srows : srows + 8, :] = usq
        each(group, lambda i: send_h(k, group_peer(i)).start())

    def send_h(k, j):
        return remote(
            h_send.at[k, j], h_recv.at[k, spot], h_ssem.at[k], h_rsem.at[k],
            (zed * group + j, mz),
        )

    def send_z(k, j):
        return remote(
            z_recv.at[k, zed], z_recv.at[k, zed], z_ssem.at[k], z_rsem.at[k],
            (j * group + spot, mz),
        )

    def v_rows():
        return pl.ds(pl.multiple_of(srows * spot, 8), srows)

    def send_v(k, j):
        return remote(
            vbuf.at[k, v_rows()], vbuf.at[k, v_rows()], v_ssem.at[k - 1], v_rsem.at[k - 1],
            (zed * group + j, mz),
        )

    def send_u(k, j):
        return remote(
            ubuf.at[k, my_rows()], ubuf.at[k, my_rows()], u_ssem.at[k - 1], u_rsem.at[k - 1],
            (pix, j),
        )

    gradients(0)

    down_copy.wait()
    q_col = lax.broadcasted_iota(jnp.int32, (piece, cols), 0) // rows + pairs * mz
    q_row = lax.broadcasted_iota(jnp.int32, (piece, cols), 0) % rows
    col = lax.broadcasted_iota(jnp.int32, (piece, cols), 1)
    p_col = lax.broadcasted_iota(jnp.int32, (cols, 128), 0)
    p_half = lax.broadcasted_iota(jnp.int32, (cols, 128), 1) // 64

    def spread(which, keep, offset):
        pick = jnp.where(keep & ((col + offset) // 2 == q_col), wtmp[...], 0.0)
        place = jnp.where((p_col + offset) % 2 == p_half, 0.25, 0.0)
        weights[which] = mm(pick.astype(BF16), place.astype(BF16))

    levels = across_in[...].astype(F32) + 1.0
    for t in range(pairs):
        wtmp[rows * t : rows * (t + 1), :] = levels
    spread(0, col < cols - 1, 0)
    spread(1, col < cols - 1, 1)
    levels = down_in[...].astype(F32) + 1.0
    for t in range(pairs):
        wtmp[rows * t : rows * (t + 1), :] = levels
    spread(2, (q_row < rows - 1) | (pix < n_pix - 1), 0)
    for t in range(pairs):
        wtmp[rows * t : rows * t + 1, :] = down_above[rows - 1 : rows, :].astype(F32) + 1.0
        wtmp[rows * t + 1 : rows * (t + 1), :] = levels[0 : rows - 1, :]
    spread(3, (q_row > 0) | (pix > 0), 0)

    smooth = jnp.concatenate([smooth_in[...], smooth_in[...]], axis=1)
    lane = lax.broadcasted_iota(jnp.int32, (piece, 128), 1)

    def laplace(k):
        for copy in halos(k):
            copy.wait()
        window = ubuf[k, pl.ds(pl.multiple_of(piece * mz, 8), piece + 16), :]
        mine = window[8 : 8 + piece]
        swapped = pltpu.roll(mine, 64, 1)
        before = pltpu.roll(window[8 - rows : 8 - rows + piece], 64, 1)
        after = pltpu.roll(window[8 + rows : 8 + rows + piece], 64, 1)
        right = jnp.where(lane < 64, swapped, after)
        left = jnp.where(lane < 64, before, swapped)
        shift[0] = window[7 : 7 + piece]
        shift[1] = window[9 : 9 + piece]
        shift[0, pl.ds(0, pairs, stride=rows), :] = halo_recv[k, 0]
        shift[1, pl.ds(rows - 1, pairs, stride=rows), :] = halo_recv[k, 1]
        flow = weights[0] * (mine - right) + weights[1] * (mine - left)
        flow = flow + weights[2] * (mine - shift[1]) + weights[3] * (mine - shift[0])
        return mine, flow * smooth

    for k in range(ITERS):
        mine, lap = laplace(k)
        drain(h_recv.at[k, pl.ds(0, group - 1)], h_rsem.at[k])
        h_recv[k, spot] = h_send[k, spot]
        total = h_recv[k, 0]
        for j in range(1, group):
            total = total + h_recv[k, j]
        z_recv[k, zed] = total
        each(n_z, lambda i: send_z(k, z_peer(i)).start())
        drain(z_recv.at[k, pl.ds(0, n_z - 1)], z_rsem.at[k])
        total = z_recv[k, 0]
        for j in range(1, n_z):
            total = total + z_recv[k, j]
        usq = jnp.sum(total[srows:, :])
        eta_v = 1.0 / (jnp.full((1, 128), usq, F32) / rank + 1.0)
        vbuf[k + 1, v_rows(), :] = vbuf[k, v_rows(), :] - eta_v * total[0:srows, :]
        each(group, lambda i: send_v(k + 1, group_peer(i)).start())
        drain(g_recv.at[k, pl.ds(0, n_mz - 1)], g_rsem.at[k])
        g_recv[k, mz] = g_send[k, mz]
        total = g_recv[k, 0]
        for j in range(1, n_mz):
            total = total + g_recv[k, j]
        vsq = jnp.sum(total[piece:, :])
        eta_u = 1.0 / (jnp.full((1, 128), vsq, F32) / rank + 8.0 * smooth + 1.0)
        mine = mine - eta_u * (total[0:piece, :] + lap)
        ubuf[k + 1, my_rows(), :] = mine
        each(n_mz, lambda i: send_u(k + 1, mz_peer(i)).start())
        if k + 1 < ITERS:
            send_halos(k + 1, mine)
        drain(vbuf.at[k + 1, pl.ds(0, srows * (group - 1))], v_rsem.at[k])
        drain(ubuf.at[k + 1, pl.ds(8, piece * (n_mz - 1))], u_rsem.at[k])
        if k + 1 < ITERS:
            gradients(k + 1)

    for t in range(cols // 2):
        u_in[:, 128 * t : 128 * (t + 1)] = ubuf[ITERS, 8 + rows * t : 8 + rows * (t + 1), :]
    out_u = pltpu.make_async_copy(u_in, uo_hbm, out_sems.at[0])
    out_u.start()
    v_in[...] = vbuf[ITERS].T
    out_v = pltpu.make_async_copy(v_in, vo_hbm, out_sems.at[1])
    out_v.start()
    sweep(ITERS)
    for r in range(rows):
        for par, src in ((0, c_e), (1, c_o)):
            xf[pl.ds(r * cols + par, cols // 2, stride=2), :] = src[
                pl.ds(r, cols // 2, stride=rows), :
            ]
    x_in[...] = xf[...].astype(BF16).reshape(rows, cols, bins)
    out_s = pltpu.make_async_copy(x_in, so_hbm, out_sems.at[2])
    out_s.start()

    for k in range(ITERS):
        drain(g_send.at[k, pl.ds(0, n_mz - 1)], g_ssem.at[k])
        drain(h_send.at[k, pl.ds(0, group - 1)], h_ssem.at[k])
        drain(z_recv.at[k, pl.ds(0, n_z - 1)], z_ssem.at[k])
        drain(vbuf.at[k, pl.ds(0, srows * (group - 1))], v_ssem.at[k])
        drain(ubuf.at[k, pl.ds(8, piece * (n_mz - 1))], u_ssem.at[k])
    out_u.wait()
    out_v.wait()
    out_s.wait()


def shards(group, spectra, scores, loadings, smooth, thresholds, across, down):
    rows, cols, bins = spectra.shape
    rank = loadings.shape[1]
    n_pix, n_mz = lax.axis_size("pix"), lax.axis_size("mz")
    nq = rows * cols // 2
    piece = nq // n_mz
    pairs = piece // rows
    srows = rank // group
    n_z = n_pix // group
    anywhere = pl.BlockSpec(memory_space=pl.ANY)
    dma = pltpu.SemaphoreType.DMA
    vmem = pltpu.VMEM
    args = (
        spectra, scores, loadings, smooth.reshape(1, rank), thresholds.reshape(1, bins),
        across, down,
    )
    return pl.pallas_call(
        functools.partial(kernel, group),
        out_shape=(
            jax.ShapeDtypeStruct(scores.shape, F32),
            jax.ShapeDtypeStruct(loadings.shape, F32),
            jax.ShapeDtypeStruct(spectra.shape, BF16),
        ),
        in_specs=[anywhere] * 7,
        out_specs=(anywhere,) * 3,
        scratch_shapes=[
            vmem(spectra.shape, BF16),
            vmem(scores.shape, F32),
            vmem(loadings.shape, F32),
            vmem((1, rank), F32),
            vmem((1, bins), F32),
            vmem(across.shape, jnp.int32),
            vmem(down.shape, jnp.int32),
            vmem(down.shape, jnp.int32),
            vmem((rows * cols, bins), F32),
            vmem((nq, bins), F32),
            vmem((nq, bins), F32),
            vmem((nq, bins), F32),
            vmem((nq, bins), F32),
            vmem((nq, 256), BF16),
            vmem((nq, 2 * bins), BF16),
            vmem((nq, 2 * bins), BF16),
            vmem((256, 2 * bins), BF16),
            vmem((256, 2 * bins), BF16),
            vmem((ITERS + 1, nq + 16, 128), F32),
            vmem((ITERS + 1, rank, bins), F32),
            vmem((ITERS, n_mz, piece + 1, 128), F32),
            vmem((ITERS, n_mz, piece + 1, 128), F32),
            vmem((ITERS, group, srows + 8, 128), F32),
            vmem((ITERS, group, srows + 8, 128), F32),
            vmem((ITERS, n_z, srows + 8, 128), F32),
            vmem((ITERS, 2, pairs, 128), F32),
            vmem((ITERS, 2, pairs, 128), F32),
            vmem((piece, cols), F32),
            vmem((2, piece, 128), F32),
            vmem((4, piece, 128), F32),
            dma((7,)),
            dma((3,)),
            dma((ITERS,)),
            dma((ITERS,)),
            dma((ITERS,)),
            dma((ITERS,)),
            dma((ITERS,)),
            dma((ITERS,)),
            dma((ITERS,)),
            dma((ITERS,)),
            dma((ITERS,)),
            dma((ITERS,)),
            dma((ITERS, 2)),
            dma((ITERS, 2)),
            dma,
            dma,
        ],
        compiler_params=pltpu.CompilerParams(
            collective_id=0, has_side_effects=True, vmem_limit_bytes=32 * 1024 * 1024
        ),
        cost_estimate=pl.CostEstimate(
            flops=2 * 10 * rows * cols * bins * rank * 3,
            bytes_accessed=2 * (spectra.size * 2 + scores.size * 4),
            transcendentals=0,
        ),
    )(*args)


def solution(mesh, group=GROUP):
    in_specs = (
        P("pix", None, "mz"),
        P("pix", None),
        P("mz", None),
        P(),
        P("mz"),
        P("pix", None),
        P("pix", None),
    )
    out_specs = (P("pix", None), P("mz", None), P("pix", None, "mz"))
    return jax.shard_map(
        functools.partial(shards, group), mesh=mesh, in_specs=in_specs, out_specs=out_specs,
        check_vma=False,
    )
```

```python
import functools
import jax
import jax.numpy as jnp
from jax import lax
from jax.experimental import pallas as pl
from jax.experimental.pallas import tpu as pltpu
from jax.sharding import PartitionSpec as P

ITERS = 3
GROUP = 8
MESH = pl.DeviceIdType.MESH
F32 = jnp.float32
BF16 = jnp.bfloat16
NT = (((1,), (1,)), ((), ()))
TN = (((0,), (0,)), ((), ()))


def mm(a, b, dims=(((1,), (0,)), ((), ()))):
    return lax.dot_general(a, b, dims, preferred_element_type=F32)


def split(a):
    high = a.astype(BF16)
    return high, (a - high.astype(F32)).astype(BF16)


def kernel(
    group,
    x_hbm, u_hbm, v_hbm, smooth_hbm, thr_hbm, across_hbm, down_hbm,
    uo_ref, vo_ref, so_ref,
    x_in, u_in, v_in, smooth_in, thr_in, across_in, down_in, down_above,
    xf, x_own, x_other, c_own, c_other, u_hl, d_h, d_l, b_hh, b_hl, ubuf, vbuf, thr_other,
    g_send, g_recv, h_send, h_recv, z_recv, halo_send, halo_recv,
    wtmp, shift, weights,
    in_sems, out_sems, g_ssem, g_rsem, u_ssem, u_rsem, h_ssem, h_rsem, z_ssem, z_rsem,
    v_ssem, v_rsem, halo_ssem, halo_rsem, down_ssem, down_rsem, thr_ssem, thr_rsem,
    x_ssem, x_rsem, c_ssem, c_rsem,
):
    n_pix, n_mz = lax.axis_size("pix"), lax.axis_size("mz")
    pix, mz = lax.axis_index("pix"), lax.axis_index("mz")
    n_z, n_y, n_team = n_pix // group, n_mz // 2, 2 * group
    zed, spot = pix // group, pix % group
    y, side = mz // 2, mz % 2
    strip, seat = side * n_y + y, side * group + spot
    twin = (pix, 2 * y + 1 - side)
    rows, cols, bins = x_in.shape
    rank = v_in.shape[0]
    nq = rows * cols // 2
    half = nq // 2
    piece = nq // n_mz
    pairs = piece // rows
    srows = rank // group
    below, above = (pix + 1) % n_pix, (pix + n_pix - 1) % n_pix

    barrier = pltpu.get_barrier_semaphore()

    def greet(device):
        pl.semaphore_signal(barrier, inc=1, device_id=device, device_id_type=MESH)

    def each(count, act):
        lax.fori_loop(0, count, lambda i, _: (act(i), 0)[1], 0)

    def far_first(at, i, n):
        return (at + n // 2 + ((i + 1) // 2) * (1 - 2 * (i % 2)) + n) % n

    def y_peer(i):
        return far_first(y, i, n_y)

    def mz_peer(i):
        return 2 * y_peer(i // 2) + (side + 1 - i % 2) % 2

    def team_peer(i):
        return (seat + i + 1) % n_team

    def team_device(j):
        return (zed * group + j % group, 2 * y + j // group)

    def group_peer(i):
        return side * group + (spot + i + 1) % group

    def z_peer(i):
        return (zed + i + 1) % n_z

    def strip_device(j):
        return (pix, 2 * (j % n_y) + j // n_y)

    loads = [
        pltpu.make_async_copy(src, dst, in_sems.at[i])
        for i, (src, dst) in enumerate(
            [
                (u_hbm, u_in), (v_hbm, v_in), (x_hbm, x_in), (thr_hbm, thr_in),
                (down_hbm, down_in), (across_hbm, across_in), (smooth_hbm, smooth_in),
            ]
        )
    ]
    for load in loads:
        load.start()

    each(n_mz - 1, lambda i: greet((pix, mz_peer(i))))
    each(n_team - 1, lambda i: greet(team_device(team_peer(i))))
    each(n_z - 1, lambda i: greet((z_peer(i) * group + spot, mz)))
    greet((below, mz))
    greet((above, mz))

    def remote(src, dst, ssem, rsem, device):
        return pltpu.make_async_remote_copy(
            src_ref=src, dst_ref=dst, send_sem=ssem, recv_sem=rsem,
            device_id=device, device_id_type=MESH,
        )

    def drain(ref, sem):
        pltpu.make_async_copy(ref, ref, sem).wait()

    def my_rows():
        return pl.ds(pl.multiple_of(8 + piece * strip, 8), piece)

    def half_rows(which, at=0, count=half):
        return pl.ds(pl.multiple_of(half * which + at, 8), count)

    zeros8 = jnp.zeros((8, 128), F32)
    ubuf[0, 0:8, :] = zeros8
    ubuf[0, 8 + nq : 16 + nq, :] = zeros8
    b_hh[...] = jnp.zeros_like(b_hh)
    b_hl[...] = jnp.zeros_like(b_hl)
    for load in loads[:4]:
        load.wait()
    for t in range(cols // 2):
        ubuf[0, 8 + rows * t : 8 + rows * (t + 1), :] = u_in[:, 128 * t : 128 * (t + 1)]
    vbuf[0, side] = v_in[...]
    xf[...] = x_in[...].reshape(rows * cols, bins).astype(F32)
    for r in range(rows):
        for par in range(2):
            x_own[par, pl.ds(r, cols // 2, stride=rows), :] = xf[
                pl.ds(r * cols + par, cols // 2, stride=2), :
            ]

    def halos(k):
        to = ((above, mz), (below, mz), strip_device((strip + n_mz - 1) % n_mz),
              strip_device((strip + 1) % n_mz))
        return [
            remote(
                halo_send.at[k, i], halo_recv.at[k, i ^ 1], halo_ssem.at[k, i],
                halo_rsem.at[k, i ^ 1], to[i],
            )
            for i in range(2 if k == 0 else 4)
        ]

    def send_halos(k, mine):
        shift[0] = mine
        halo_send[k, 0, 0:pairs, :] = shift[0, pl.ds(0, pairs, stride=rows), :]
        halo_send[k, 1, 0:pairs, :] = shift[0, pl.ds(rows - 1, pairs, stride=rows), :]
        halo_send[k, 2, 0:8, :] = mine[0:8]
        halo_send[k, 3, 0:8, :] = mine[piece - 8 : piece]
        for copy in halos(k):
            copy.start()

    chunk = 128

    def factors(k, slot):
        high, low = split(vbuf[k, side if slot == 0 else 1 - side])
        for at, part in ((0, high), (128, high)):
            b_hh[slot, at : at + rank, 0:bins] = part
            b_hh[slot, at + rank : at + 2 * rank, bins : 2 * bins] = part
        for at, part in ((0, high), (128, low)):
            b_hl[slot, at : at + rank, 0:bins] = part
            b_hl[slot, at + rank : at + 2 * rank, bins : 2 * bins] = part

    def sweep(k):
        paired = 0 < k < ITERS
        slots = (0, 1) if paired else (0,)
        vsq = jnp.zeros((1, 128), F32)
        for slot in slots:
            factors(k, slot)
            v = vbuf[k, side if slot == 0 else 1 - side]
            vsq = vsq + jnp.sum(v * v, axis=0, keepdims=True)
        usq = zeros8
        for q in range(0, half if paired else nq, chunk):
            here = pl.ds(q, chunk)
            own = half_rows(side, q, chunk) if paired else here
            u = ubuf[k, pl.ds(pl.multiple_of(own.start + 8, 8), chunk), :]
            u_h, u_l = split(u)
            u_hl[here, 0:128] = u_h
            u_hl[here, 128:256] = u_l
            usq = usq + jnp.sum((u * u).reshape(chunk // 8, 8, 128), axis=0)
            g = None
            for slot in slots:
                approx = mm(u_hl[here, :], b_hh[slot]) + mm(u_h, b_hl[slot, 128:256, :])
                thr = (thr_other if slot else thr_in)[...]
                x, c = (x_other, c_other) if slot else (x_own, c_own)
                spot_rows = here if slot else own
                dest = pl.ds(slot * half + q, chunk)
                for par in range(2):
                    lanes = slice(par * bins, (par + 1) * bins)
                    low = approx[:, lanes]
                    data = x[par, spot_rows, :]
                    if k == 0:
                        d = low - data
                    else:
                        t = data - low
                        if k > 1:
                            old = c[par, spot_rows, :]
                            t = t + old
                        clipped = jnp.clip(t, -thr, thr)
                        if k == ITERS:
                            c[par, spot_rows, :] = t - clipped
                            continue
                        c[par, spot_rows, :] = clipped
                        d = -2.0 * clipped
                        if k > 1:
                            d = d + old
                    high, low = split(d)
                    d_h[dest, lanes] = high
                    d_l[dest, lanes] = low
                if k == ITERS:
                    continue
                g2 = mm(d_h[dest, :], b_hl[slot], NT)
                part = g2[:, 0:128] + g2[:, 128:256] + mm(d_l[dest, :], b_hh[slot, 0:128, :], NT)
                g = part if g is None else g + part
            if k == ITERS:
                continue
            for j in range(q // piece, (q + chunk) // piece):
                g_send[k, j, 0:piece, :] = g[j * piece - q : (j + 1) * piece - q, :]
                g_send[k, j, piece : piece + 1, :] = vsq
        return usq

    def send_g(k, i):
        if k == 0:
            to = mz_peer(i)
            return remote(
                g_send.at[k, (to % 2) * n_y + to // 2], g_recv.at[k, mz], g_ssem.at[k],
                g_rsem.at[k], (pix, to),
            )
        to = y_peer(i)
        return remote(
            g_send.at[k, to], g_recv.at[k, y], g_ssem.at[k], g_rsem.at[k], (pix, 2 * to + side)
        )

    def send_h(k, j):
        return remote(
            h_send.at[k, j], h_recv.at[k, seat], h_ssem.at[k], h_rsem.at[k], team_device(j)
        )

    def send_z(k, j):
        return remote(
            z_recv.at[k, zed], z_recv.at[k, zed], z_ssem.at[k], z_rsem.at[k],
            (j * group + spot, mz),
        )

    def v_rows():
        return pl.ds(pl.multiple_of(srows * spot, 8), srows)

    def send_v(k, j):
        ref = vbuf.at[k, side, v_rows()]
        return remote(ref, ref, v_ssem.at[k - 1], v_rsem.at[k - 1], team_device(j))

    def send_u(k, to):
        ref = ubuf.at[k, my_rows()]
        return remote(ref, ref, u_ssem.at[k - 1], u_rsem.at[k - 1], (pix, to))

    def g_count(k):
        return n_mz if k == 0 else n_y

    def h_count(k):
        return group if k == 0 else n_team

    def u_count(k):
        return n_mz if k == ITERS else n_y

    def v_count(k):
        return group if k == ITERS else n_team

    def start_g(k):
        each(g_count(k) - 1, lambda i: send_g(k, i).start())

    def h_part(k, usq):
        for slot in (0,) if k == 0 else (0, 1):
            n = nq if k == 0 else half
            dest = slice(slot * half, slot * half + n)
            both = mm(u_hl[0:n, :], d_h[dest, :], TN)
            prod = both[0:128, :] + both[128:256, :] + mm(u_hl[0:n, 0:128], d_l[dest, :], TN)
            h = prod[0:rank, 0:bins] + prod[rank : 2 * rank, bins : 2 * bins]
            whose = side if slot == 0 else 1 - side
            for j in range(group):
                h_send[k, whose * group + j, 0:srows, :] = h[j * srows : (j + 1) * srows, :]
                h_send[k, whose * group + j, srows : srows + 8, :] = usq
        peer = group_peer if k == 0 else team_peer
        each(h_count(k) - 1, lambda i: send_h(k, peer(i)).start())

    usq = sweep(0)

    pl.semaphore_wait(barrier, n_mz - 1 + n_team - 1 + n_z - 1 + 2)
    start_g(0)
    h_part(0, usq)
    send_halos(0, ubuf[0, my_rows(), :])
    thr_copy = remote(thr_in, thr_other, thr_ssem, thr_rsem, twin)
    thr_copy.start()
    loads[4].wait()
    down_copy = remote(down_in, down_above, down_ssem, down_rsem, (below, mz))
    down_copy.start()
    x_copies = [
        remote(
            x_own.at[par, half_rows(1 - side)], x_other.at[par], x_ssem.at[par], x_rsem.at[par],
            twin,
        )
        for par in range(2)
    ]
    for copy in x_copies:
        copy.start()
    c_copies = [
        remote(
            c_other.at[par], c_own.at[par, half_rows(side)], c_ssem.at[par], c_rsem.at[par],
            twin,
        )
        for par in range(2)
    ]

    for load in loads[5:]:
        load.wait()
    q_col = lax.broadcasted_iota(jnp.int32, (piece, cols), 0) // rows + pairs * strip
    q_row = lax.broadcasted_iota(jnp.int32, (piece, cols), 0) % rows
    col = lax.broadcasted_iota(jnp.int32, (piece, cols), 1)
    p_col = lax.broadcasted_iota(jnp.int32, (cols, 128), 0)
    p_half = lax.broadcasted_iota(jnp.int32, (cols, 128), 1) // 64

    def spread(which, keep, offset):
        pick = jnp.where(keep & ((col + offset) // 2 == q_col), wtmp[...], 0.0)
        place = jnp.where((p_col + offset) % 2 == p_half, 0.25, 0.0)
        weights[which] = mm(pick.astype(BF16), place.astype(BF16))

    levels = across_in[...].astype(F32) + 1.0
    for t in range(pairs):
        wtmp[rows * t : rows * (t + 1), :] = levels
    spread(0, col < cols - 1, 0)
    spread(1, col < cols - 1, 1)
    levels = down_in[...].astype(F32) + 1.0
    for t in range(pairs):
        wtmp[rows * t : rows * (t + 1), :] = levels
    spread(2, (q_row < rows - 1) | (pix < n_pix - 1), 0)
    down_copy.wait()
    for t in range(pairs):
        wtmp[rows * t : rows * t + 1, :] = down_above[rows - 1 : rows, :].astype(F32) + 1.0
        wtmp[rows * t + 1 : rows * (t + 1), :] = levels[0 : rows - 1, :]
    spread(3, (q_row > 0) | (pix > 0), 0)

    smooth = jnp.concatenate([smooth_in[...], smooth_in[...]], axis=1)
    lane = lax.broadcasted_iota(jnp.int32, (piece, 128), 1)

    def laplace(k):
        for copy in halos(k):
            copy.wait()
        if k == 0:
            window = ubuf[k, pl.ds(pl.multiple_of(piece * strip, 8), piece + 16), :]
        else:
            window = jnp.concatenate(
                [halo_recv[k, 2, 0:8, :], ubuf[k, my_rows(), :], halo_recv[k, 3, 0:8, :]], axis=0
            )
        mine = window[8 : 8 + piece]
        swapped = pltpu.roll(mine, 64, 1)
        before = pltpu.roll(window[8 - rows : 8 - rows + piece], 64, 1)
        after = pltpu.roll(window[8 + rows : 8 + rows + piece], 64, 1)
        right = jnp.where(lane < 64, swapped, after)
        left = jnp.where(lane < 64, before, swapped)
        shift[0] = window[7 : 7 + piece]
        shift[1] = window[9 : 9 + piece]
        shift[0, pl.ds(0, pairs, stride=rows), :] = halo_recv[k, 0, 0:pairs, :]
        shift[1, pl.ds(rows - 1, pairs, stride=rows), :] = halo_recv[k, 1, 0:pairs, :]
        flow = weights[0] * (mine - right) + weights[1] * (mine - left)
        flow = flow + weights[2] * (mine - shift[1]) + weights[3] * (mine - shift[0])
        return mine, flow * smooth

    for k in range(ITERS):
        mine, lap = laplace(k)
        drain(h_recv.at[k, pl.ds(0, h_count(k) - 1)], h_rsem.at[k])
        h_recv[k, seat] = h_send[k, seat]
        first = side * group if k == 0 else 0
        total = h_recv[k, first]
        for j in range(1, h_count(k)):
            total = total + h_recv[k, first + j]
        z_recv[k, zed] = total
        each(n_z - 1, lambda i: send_z(k, z_peer(i)).start())
        if k == ITERS - 1:
            for copy in c_copies:
                copy.start()
        drain(g_recv.at[k, pl.ds(0, g_count(k) - 1)], g_rsem.at[k])
        if k == 0:
            g_recv[k, mz] = g_send[k, strip]
        else:
            g_recv[k, y] = g_send[k, y]
        total = g_recv[k, 0]
        for j in range(1, g_count(k)):
            total = total + g_recv[k, j]
        vsq = jnp.sum(total[piece:, :])
        eta_u = 1.0 / (jnp.full((1, 128), vsq, F32) / rank + 8.0 * smooth + 1.0)
        mine = mine - eta_u * (total[0:piece, :] + lap)
        ubuf[k + 1, my_rows(), :] = mine
        if k + 1 < ITERS:
            each(n_y - 1, lambda i: send_u(k + 1, 2 * y_peer(i) + side).start())
            send_halos(k + 1, mine)
        else:
            each(n_mz - 1, lambda i: send_u(k + 1, mz_peer(i)).start())
        drain(z_recv.at[k, pl.ds(0, n_z - 1)], z_rsem.at[k])
        total = z_recv[k, 0]
        for j in range(1, n_z):
            total = total + z_recv[k, j]
        usq = jnp.sum(total[srows:, :])
        eta_v = 1.0 / (jnp.full((1, 128), usq, F32) / rank + 1.0)
        vbuf[k + 1, side, v_rows(), :] = vbuf[k, side, v_rows(), :] - eta_v * total[0:srows, :]
        peer = group_peer if k + 1 == ITERS else team_peer
        each(v_count(k + 1) - 1, lambda i: send_v(k + 1, peer(i)).start())
        if k == 0:
            thr_copy.wait()
            for copy in x_copies:
                copy.wait()
        if k + 1 == ITERS:
            for copy in c_copies:
                copy.wait()
        drain(ubuf.at[0, pl.ds(0, srows * (v_count(k + 1) - 1))], v_rsem.at[k])
        drain(ubuf.at[k + 1, pl.ds(8, piece * (u_count(k + 1) - 1))], u_rsem.at[k])
        if k + 1 < ITERS:
            usq = sweep(k + 1)
            start_g(k + 1)
            h_part(k + 1, usq)

    for t in range(cols // 2):
        u_in[:, 128 * t : 128 * (t + 1)] = ubuf[ITERS, 8 + rows * t : 8 + rows * (t + 1), :]
    v_in[...] = vbuf[ITERS, side]
    outs = [
        pltpu.make_async_copy(src, dst, out_sems.at[i])
        for i, (src, dst) in enumerate([(u_in, uo_ref), (v_in, vo_ref), (x_in, so_ref)])
    ]
    outs[0].start()
    outs[1].start()
    sweep(ITERS)
    for r in range(rows):
        for par in range(2):
            xf[pl.ds(r * cols + par, cols // 2, stride=2), :] = c_own[
                par, pl.ds(r, cols // 2, stride=rows), :
            ]
    x_in[...] = xf[...].astype(BF16).reshape(rows, cols, bins)
    outs[2].start()

    for k in range(ITERS):
        drain(g_send.at[k, pl.ds(0, g_count(k) - 1)], g_ssem.at[k])
        drain(h_send.at[k, pl.ds(0, h_count(k) - 1)], h_ssem.at[k])
        drain(z_recv.at[k, pl.ds(0, n_z - 1)], z_ssem.at[k])
        drain(ubuf.at[0, pl.ds(0, srows * (v_count(k + 1) - 1))], v_ssem.at[k])
        drain(ubuf.at[k + 1, pl.ds(8, piece * (u_count(k + 1) - 1))], u_ssem.at[k])
    for out in outs:
        out.wait()


def shards(group, spectra, scores, loadings, smooth, thresholds, across, down):
    rows, cols, bins = spectra.shape
    rank = loadings.shape[1]
    n_pix, n_mz = lax.axis_size("pix"), lax.axis_size("mz")
    nq = rows * cols // 2
    half = nq // 2
    piece = nq // n_mz
    edge = max(piece // rows, 8)
    srows = rank // group
    n_z, n_team = n_pix // group, 2 * group
    hbm = pl.BlockSpec(memory_space=pltpu.HBM)
    anywhere = pl.BlockSpec(memory_space=pl.ANY)
    dma = pltpu.SemaphoreType.DMA
    vmem = pltpu.VMEM
    args = (
        spectra, scores, loadings.T, smooth.reshape(1, rank), thresholds.reshape(1, bins),
        across, down,
    )
    out_shape = (
        jax.ShapeDtypeStruct(scores.shape, F32),
        jax.ShapeDtypeStruct((rank, bins), F32),
        jax.ShapeDtypeStruct(spectra.shape, BF16),
    )
    score_maps, final, sparse = pl.pallas_call(
        functools.partial(kernel, group),
        out_shape=out_shape,
        in_specs=[hbm] * 7,
        out_specs=(anywhere,) * 3,
        scratch_shapes=[
            vmem(spectra.shape, BF16),
            vmem(scores.shape, F32),
            vmem((rank, bins), F32),
            vmem((1, rank), F32),
            vmem((1, bins), F32),
            vmem(across.shape, jnp.int32),
            vmem(down.shape, jnp.int32),
            vmem(down.shape, jnp.int32),
            vmem((rows * cols, bins), F32),
            vmem((2, nq, bins), F32),
            vmem((2, half, bins), F32),
            vmem((2, nq, bins), F32),
            vmem((2, half, bins), F32),
            vmem((nq, 256), BF16),
            vmem((nq, 2 * bins), BF16),
            vmem((nq, 2 * bins), BF16),
            vmem((2, 256, 2 * bins), BF16),
            vmem((2, 256, 2 * bins), BF16),
            vmem((ITERS + 1, nq + 16, 128), F32),
            vmem((ITERS + 1, 2, rank, bins), F32),
            vmem((1, bins), F32),
            vmem((ITERS, n_mz, piece + 1, 128), F32),
            vmem((ITERS, n_mz, piece + 1, 128), F32),
            vmem((ITERS, n_team, srows + 8, 128), F32),
            vmem((ITERS, n_team, srows + 8, 128), F32),
            vmem((ITERS, n_z, srows + 8, 128), F32),
            vmem((ITERS, 4, edge, 128), F32),
            vmem((ITERS, 4, edge, 128), F32),
            vmem((piece, cols), F32),
            vmem((2, piece, 128), F32),
            vmem((4, piece, 128), F32),
            dma((7,)),
            dma((3,)),
        ]
        + [dma((ITERS,))] * 10
        + [dma((ITERS, 4))] * 2
        + [dma] * 4
        + [dma((2,))] * 4,
        compiler_params=pltpu.CompilerParams(
            collective_id=0, has_side_effects=True, vmem_limit_bytes=63 * 1024 * 1024
        ),
        cost_estimate=pl.CostEstimate(
            flops=2 * 10 * rows * cols * bins * rank * 3,
            bytes_accessed=2 * (spectra.size * 2 + scores.size * 4),
            transcendentals=0,
        ),
    )(*args)
    return score_maps, final.T, sparse


def solution(mesh, group=GROUP):
    in_specs = (
        P("pix", None, "mz"),
        P("pix", None),
        P("mz", None),
        P(),
        P("mz"),
        P("pix", None),
        P("pix", None),
    )
    out_specs = (P("pix", None), P("mz", None), P("pix", None, "mz"))
    return jax.shard_map(
        functools.partial(shards, group), mesh=mesh, in_specs=in_specs, out_specs=out_specs,
        check_vma=False,
    )
```

```python
import functools
import jax
import jax.numpy as jnp
from jax import lax
from jax.experimental import pallas as pl
from jax.experimental.pallas import tpu as pltpu
from jax.sharding import PartitionSpec as P

ITERS = 3
GROUP = 8
MESH = pl.DeviceIdType.MESH
F32 = jnp.float32
BF16 = jnp.bfloat16
NT = (((1,), (1,)), ((), ()))
TN = (((0,), (0,)), ((), ()))


def mm(a, b, dims=(((1,), (0,)), ((), ()))):
    return lax.dot_general(a, b, dims, preferred_element_type=F32)


def split(a):
    high = a.astype(BF16)
    return high, (a - high.astype(F32)).astype(BF16)


def kernel(
    group,
    x_hbm, u_hbm, v_hbm, smooth_hbm, thr_hbm, across_hbm, down_hbm,
    uo_ref, vo_ref, so_ref,
    x_in, u_in, v_in, smooth_in, thr_in, across_in, down_in, down_above,
    xf, x_own, x_other, c_own, c_other, u_hl, d_h, d_l, b_hh, b_hl, ubuf, vbuf, thr_other,
    g_send, g_recv, h_send, h_recv, z_recv, halo_send, halo_recv,
    wtmp, shift, weights,
    in_sems, out_sems, g_ssem, g_rsem, u_ssem, u_rsem, h_ssem, h_rsem, z_ssem, z_rsem,
    v_ssem, v_rsem, halo_ssem, halo_rsem, down_ssem, down_rsem, thr_ssem, thr_rsem,
    x_ssem, x_rsem, c_ssem, c_rsem, cross_rsem,
):
    n_pix, n_mz = lax.axis_size("pix"), lax.axis_size("mz")
    pix, mz = lax.axis_index("pix"), lax.axis_index("mz")
    n_z, n_y, n_team = n_pix // group, n_mz // 2, 2 * group
    zed, spot = pix // group, pix % group
    y, side = mz // 2, mz % 2
    strip, seat = side * n_y + y, side * group + spot
    twin = (pix, 2 * y + 1 - side)
    rows, cols, bins = x_in.shape
    rank = v_in.shape[0]
    nq = rows * cols // 2
    half = nq // 2
    piece = nq // n_mz
    pairs = piece // rows
    srows = rank // group
    below, above = (pix + 1) % n_pix, (pix + n_pix - 1) % n_pix

    barrier = pltpu.get_barrier_semaphore()

    def greet(device):
        pl.semaphore_signal(barrier, inc=1, device_id=device, device_id_type=MESH)

    def each(count, act):
        lax.fori_loop(0, count, lambda i, _: (act(i), 0)[1], 0)

    def far_first(at, i, n):
        return (at + n // 2 + ((i + 1) // 2) * (1 - 2 * (i % 2)) + n) % n

    def y_peer(i):
        return far_first(y, i, n_y)

    def mz_peer(i):
        return 2 * y_peer(i // 2) + (side + 1 - i % 2) % 2

    def team_peer(i):
        return (seat + i + 1) % n_team

    def team_device(j):
        return (zed * group + j % group, 2 * y + j // group)

    def group_peer(i):
        return side * group + (spot + i + 1) % group

    def z_peer(i):
        return (zed + i + 1) % n_z

    def strip_device(j):
        return (pix, 2 * (j % n_y) + j // n_y)

    loads = [
        pltpu.make_async_copy(src, dst, in_sems.at[i])
        for i, (src, dst) in enumerate(
            [
                (u_hbm, u_in), (v_hbm, v_in), (x_hbm, x_in), (thr_hbm, thr_in),
                (down_hbm, down_in), (across_hbm, across_in), (smooth_hbm, smooth_in),
            ]
        )
    ]
    for load in loads:
        load.start()

    each(n_mz - 1, lambda i: greet((pix, mz_peer(i))))
    each(n_team - 1, lambda i: greet(team_device(team_peer(i))))
    each(n_z - 1, lambda i: greet((z_peer(i) * group + spot, mz)))
    greet((below, mz))
    greet((above, mz))

    def remote(src, dst, ssem, rsem, device):
        return pltpu.make_async_remote_copy(
            src_ref=src, dst_ref=dst, send_sem=ssem, recv_sem=rsem,
            device_id=device, device_id_type=MESH,
        )

    def drain(ref, sem):
        pltpu.make_async_copy(ref, ref, sem).wait()

    def my_rows():
        return pl.ds(pl.multiple_of(8 + piece * strip, 8), piece)

    def half_rows(which, at=0, count=half):
        return pl.ds(pl.multiple_of(half * which + at, 8), count)

    zeros8 = jnp.zeros((8, 128), F32)
    ubuf[0, 0:8, :] = zeros8
    ubuf[0, 8 + nq : 16 + nq, :] = zeros8
    b_hh[...] = jnp.zeros_like(b_hh)
    b_hl[...] = jnp.zeros_like(b_hl)
    for load in loads[:4]:
        load.wait()
    for t in range(cols // 2):
        ubuf[0, 8 + rows * t : 8 + rows * (t + 1), :] = u_in[:, 128 * t : 128 * (t + 1)]
    vbuf[0, side] = v_in[...]
    xf[...] = x_in[...].reshape(rows * cols, bins).astype(F32)
    for r in range(rows):
        for par in range(2):
            x_own[par, pl.ds(r, cols // 2, stride=rows), :] = xf[
                pl.ds(r * cols + par, cols // 2, stride=2), :
            ]

    def halos(k):
        to = ((above, mz), (below, mz), strip_device((strip + n_mz - 1) % n_mz),
              strip_device((strip + 1) % n_mz))
        return [
            remote(
                halo_send.at[k, i], halo_recv.at[k, i ^ 1], halo_ssem.at[k, i],
                halo_rsem.at[k, i ^ 1], to[i],
            )
            for i in range(2 if k == 0 else 4)
        ]

    def send_halos(k, mine):
        shift[0] = mine
        halo_send[k, 0, 0:pairs, :] = shift[0, pl.ds(0, pairs, stride=rows), :]
        halo_send[k, 1, 0:pairs, :] = shift[0, pl.ds(rows - 1, pairs, stride=rows), :]
        halo_send[k, 2, 0:8, :] = mine[0:8]
        halo_send[k, 3, 0:8, :] = mine[piece - 8 : piece]
        for copy in halos(k):
            copy.start()

    chunk = 128

    def factors(k, slot):
        high, low = split(vbuf[k, side if slot == 0 else 1 - side])
        for at, part in ((0, high), (128, high)):
            b_hh[slot, at : at + rank, 0:bins] = part
            b_hh[slot, at + rank : at + 2 * rank, bins : 2 * bins] = part
        for at, part in ((0, high), (128, low)):
            b_hl[slot, at : at + rank, 0:bins] = part
            b_hl[slot, at + rank : at + 2 * rank, bins : 2 * bins] = part

    def sweep(k, which=None):
        paired = 0 < k < ITERS
        slots = (0, 1) if paired else (0,)
        vsq = jnp.zeros((1, 128), F32)
        for slot in slots if which is None or which is side else ():
            factors(k, slot)
            v = vbuf[k, side if slot == 0 else 1 - side]
            vsq = vsq + jnp.sum(v * v, axis=0, keepdims=True)
        usq = zeros8
        for q in range(0, nq if k == 0 else half, chunk):
            here = pl.ds(q, chunk)
            own = here if k == 0 else half_rows(side if which is None else which, q, chunk)
            u = ubuf[k, pl.ds(pl.multiple_of(own.start + 8, 8), chunk), :]
            u_h, u_l = split(u)
            u_hl[here, 0:128] = u_h
            u_hl[here, 128:256] = u_l
            usq = usq + jnp.sum((u * u).reshape(chunk // 8, 8, 128), axis=0)
            g = None
            for slot in slots:
                approx = mm(u_hl[here, :], b_hh[slot]) + mm(u_h, b_hl[slot, 128:256, :])
                thr = (thr_other if slot else thr_in)[...]
                x, c = (x_other, c_other) if slot else (x_own, c_own)
                spot_rows = here if slot else own
                dest = pl.ds(slot * half + q, chunk)
                for par in range(2):
                    lanes = slice(par * bins, (par + 1) * bins)
                    low = approx[:, lanes]
                    data = x[par, spot_rows, :]
                    if k == 0:
                        d = low - data
                    else:
                        t = data - low
                        if k > 1:
                            old = c[par, spot_rows, :]
                            t = t + old
                        clipped = jnp.clip(t, -thr, thr)
                        if k == ITERS:
                            c[par, spot_rows, :] = t - clipped
                            continue
                        c[par, spot_rows, :] = clipped
                        d = -2.0 * clipped
                        if k > 1:
                            d = d + old
                    high, low = split(d)
                    d_h[dest, lanes] = high
                    d_l[dest, lanes] = low
                if k == ITERS:
                    continue
                g2 = mm(d_h[dest, :], b_hl[slot], NT)
                part = g2[:, 0:128] + g2[:, 128:256] + mm(d_l[dest, :], b_hh[slot, 0:128, :], NT)
                g = part if g is None else g + part
            if k == ITERS:
                continue
            for j in range(q // piece, (q + chunk) // piece):
                g_send[k, j, 0:piece, :] = g[j * piece - q : (j + 1) * piece - q, :]
                g_send[k, j, piece : piece + 1, :] = vsq
        return usq

    def send_g(k, i):
        if k == 0:
            to = mz_peer(i)
            return remote(
                g_send.at[k, (to % 2) * n_y + to // 2], g_recv.at[k, mz], g_ssem.at[k],
                g_rsem.at[k], (pix, to),
            )
        to = y_peer(i)
        return remote(
            g_send.at[k, to], g_recv.at[k, y], g_ssem.at[k], g_rsem.at[k], (pix, 2 * to + side)
        )

    def send_h(k, j):
        return remote(
            h_send.at[k, j], h_recv.at[k, seat], h_ssem.at[k], h_rsem.at[k], team_device(j)
        )

    def send_z(k, j):
        return remote(
            z_recv.at[k, zed], z_recv.at[k, zed], z_ssem.at[k], z_rsem.at[k],
            (j * group + spot, mz),
        )

    def v_rows():
        return pl.ds(pl.multiple_of(srows * spot, 8), srows)

    def send_v(k, j):
        ref = vbuf.at[k, side, v_rows()]
        return remote(ref, ref, v_ssem.at[k - 1], v_rsem.at[k - 1], team_device(j))

    def send_u(k, to, rsem=None):
        ref = ubuf.at[k, my_rows()]
        rsem = u_rsem.at[k - 1] if rsem is None else rsem
        return remote(ref, ref, u_ssem.at[k - 1], rsem, (pix, to))

    def g_count(k):
        return n_mz if k == 0 else n_y

    def h_count(k):
        return group if k == 0 else n_team

    def u_count(k):
        return n_mz if k == ITERS else n_y

    def v_count(k):
        return group if k == ITERS else n_team

    def start_g(k):
        each(g_count(k) - 1, lambda i: send_g(k, i).start())

    def h_part(k, usq):
        for slot in (0,) if k == 0 else (0, 1):
            n = nq if k == 0 else half
            dest = slice(slot * half, slot * half + n)
            both = mm(u_hl[0:n, :], d_h[dest, :], TN)
            prod = both[0:128, :] + both[128:256, :] + mm(u_hl[0:n, 0:128], d_l[dest, :], TN)
            h = prod[0:rank, 0:bins] + prod[rank : 2 * rank, bins : 2 * bins]
            whose = side if slot == 0 else 1 - side
            for j in range(group):
                h_send[k, whose * group + j, 0:srows, :] = h[j * srows : (j + 1) * srows, :]
                h_send[k, whose * group + j, srows : srows + 8, :] = usq
        peer = group_peer if k == 0 else team_peer
        each(h_count(k) - 1, lambda i: send_h(k, peer(i)).start())

    usq = sweep(0)
    pl.semaphore_wait(barrier, n_mz - 1 + n_team - 1 + n_z - 1 + 2)
    x_copies = [
        remote(
            x_own.at[par, half_rows(1 - side)], x_other.at[par], x_ssem.at[par], x_rsem.at[par],
            twin,
        )
        for par in range(2)
    ]
    start_g(0)
    h_part(0, usq)
    send_halos(0, ubuf[0, my_rows(), :])
    thr_copy = remote(thr_in, thr_other, thr_ssem, thr_rsem, twin)
    thr_copy.start()
    loads[4].wait()
    down_copy = remote(down_in, down_above, down_ssem, down_rsem, (below, mz))
    down_copy.start()
    c_copies = [
        remote(
            c_other.at[par], c_own.at[par, half_rows(side)], c_ssem.at[par], c_rsem.at[par],
            twin,
        )
        for par in range(2)
    ]

    for load in loads[5:]:
        load.wait()
    q_col = lax.broadcasted_iota(jnp.int32, (piece, cols), 0) // rows + pairs * strip
    q_row = lax.broadcasted_iota(jnp.int32, (piece, cols), 0) % rows
    col = lax.broadcasted_iota(jnp.int32, (piece, cols), 1)
    p_col = lax.broadcasted_iota(jnp.int32, (cols, 128), 0)
    p_half = lax.broadcasted_iota(jnp.int32, (cols, 128), 1) // 64

    def spread(which, keep, offset):
        pick = jnp.where(keep & ((col + offset) // 2 == q_col), wtmp[...], 0.0)
        place = jnp.where((p_col + offset) % 2 == p_half, 0.25, 0.0)
        weights[which] = mm(pick.astype(BF16), place.astype(BF16))

    levels = across_in[...].astype(F32) + 1.0
    for t in range(pairs):
        wtmp[rows * t : rows * (t + 1), :] = levels
    spread(0, col < cols - 1, 0)
    spread(1, col < cols - 1, 1)
    levels = down_in[...].astype(F32) + 1.0
    for t in range(pairs):
        wtmp[rows * t : rows * (t + 1), :] = levels
    spread(2, (q_row < rows - 1) | (pix < n_pix - 1), 0)
    down_copy.wait()
    for t in range(pairs):
        wtmp[rows * t : rows * t + 1, :] = down_above[rows - 1 : rows, :].astype(F32) + 1.0
        wtmp[rows * t + 1 : rows * (t + 1), :] = levels[0 : rows - 1, :]
    spread(3, (q_row > 0) | (pix > 0), 0)

    smooth = jnp.concatenate([smooth_in[...], smooth_in[...]], axis=1)
    lane = lax.broadcasted_iota(jnp.int32, (piece, 128), 1)

    def laplace(k):
        for copy in halos(k):
            copy.wait()
        if k == 0:
            window = ubuf[k, pl.ds(pl.multiple_of(piece * strip, 8), piece + 16), :]
        else:
            window = jnp.concatenate(
                [halo_recv[k, 2, 0:8, :], ubuf[k, my_rows(), :], halo_recv[k, 3, 0:8, :]], axis=0
            )
        mine = window[8 : 8 + piece]
        swapped = pltpu.roll(mine, 64, 1)
        before = pltpu.roll(window[8 - rows : 8 - rows + piece], 64, 1)
        after = pltpu.roll(window[8 + rows : 8 + rows + piece], 64, 1)
        right = jnp.where(lane < 64, swapped, after)
        left = jnp.where(lane < 64, before, swapped)
        shift[0] = window[7 : 7 + piece]
        shift[1] = window[9 : 9 + piece]
        shift[0, pl.ds(0, pairs, stride=rows), :] = halo_recv[k, 0, 0:pairs, :]
        shift[1, pl.ds(rows - 1, pairs, stride=rows), :] = halo_recv[k, 1, 0:pairs, :]
        flow = weights[0] * (mine - right) + weights[1] * (mine - left)
        flow = flow + weights[2] * (mine - shift[1]) + weights[3] * (mine - shift[0])
        return mine, flow * smooth

    for k in range(ITERS):
        mine, lap = laplace(k)
        drain(h_recv.at[k, pl.ds(0, h_count(k) - 1)], h_rsem.at[k])
        h_recv[k, seat] = h_send[k, seat]
        first = side * group if k == 0 else 0
        total = h_recv[k, first]
        for j in range(1, h_count(k)):
            total = total + h_recv[k, first + j]
        z_recv[k, zed] = total
        each(n_z - 1, lambda i: send_z(k, z_peer(i)).start())
        if k == 0:
            x_copies[0].start()
        if k == ITERS - 1:
            c_copies[1].start()
        drain(g_recv.at[k, pl.ds(0, g_count(k) - 1)], g_rsem.at[k])
        if k == 0:
            g_recv[k, mz] = g_send[k, strip]
        else:
            g_recv[k, y] = g_send[k, y]
        total = g_recv[k, 0]
        for j in range(1, g_count(k)):
            total = total + g_recv[k, j]
        vsq = jnp.sum(total[piece:, :])
        eta_u = 1.0 / (jnp.full((1, 128), vsq, F32) / rank + 8.0 * smooth + 1.0)
        mine = mine - eta_u * (total[0:piece, :] + lap)
        ubuf[k + 1, my_rows(), :] = mine
        if k + 1 < ITERS:
            each(n_y - 1, lambda i: send_u(k + 1, 2 * y_peer(i) + side).start())
            send_halos(k + 1, mine)
            if k == 0:
                x_copies[1].start()
        else:
            def both_sides(i):
                send_u(k + 1, 2 * y_peer(i) + 1 - side, cross_rsem).start()
                send_u(k + 1, 2 * y_peer(i) + side).start()

            each(n_y - 1, both_sides)
            send_u(k + 1, 2 * y + 1 - side, cross_rsem).start()
        drain(z_recv.at[k, pl.ds(0, n_z - 1)], z_rsem.at[k])
        total = z_recv[k, 0]
        for j in range(1, n_z):
            total = total + z_recv[k, j]
        usq = jnp.sum(total[srows:, :])
        eta_v = 1.0 / (jnp.full((1, 128), usq, F32) / rank + 1.0)
        vbuf[k + 1, side, v_rows(), :] = vbuf[k, side, v_rows(), :] - eta_v * total[0:srows, :]
        peer = group_peer if k + 1 == ITERS else team_peer
        each(v_count(k + 1) - 1, lambda i: send_v(k + 1, peer(i)).start())
        if k == 0:
            thr_copy.wait()
            for copy in x_copies:
                copy.wait()
        drain(ubuf.at[0, pl.ds(0, srows * (v_count(k + 1) - 1))], v_rsem.at[k])
        drain(ubuf.at[k + 1, pl.ds(8, piece * (n_y - 1))], u_rsem.at[k])
        if k + 1 < ITERS:
            usq = sweep(k + 1)
            start_g(k + 1)
            h_part(k + 1, usq)
            if k + 2 == ITERS:
                c_copies[0].start()

    sweep(ITERS, side)
    v_in[...] = vbuf[ITERS, side]
    outs = [
        pltpu.make_async_copy(src, dst, out_sems.at[i])
        for i, (src, dst) in enumerate([(u_in, uo_ref), (v_in, vo_ref), (x_in, so_ref)])
    ]
    outs[1].start()
    drain(ubuf.at[ITERS, pl.ds(8, piece * n_y)], cross_rsem)
    for copy in c_copies:
        copy.wait()
    for t in range(cols // 2):
        u_in[:, 128 * t : 128 * (t + 1)] = ubuf[ITERS, 8 + rows * t : 8 + rows * (t + 1), :]
    outs[0].start()
    sweep(ITERS, 1 - side)
    for r in range(rows):
        for par in range(2):
            xf[pl.ds(r * cols + par, cols // 2, stride=2), :] = c_own[
                par, pl.ds(r, cols // 2, stride=rows), :
            ]
    x_in[...] = xf[...].astype(BF16).reshape(rows, cols, bins)
    outs[2].start()

    for k in range(ITERS):
        drain(g_send.at[k, pl.ds(0, g_count(k) - 1)], g_ssem.at[k])
        drain(h_send.at[k, pl.ds(0, h_count(k) - 1)], h_ssem.at[k])
        drain(z_recv.at[k, pl.ds(0, n_z - 1)], z_ssem.at[k])
        drain(ubuf.at[0, pl.ds(0, srows * (v_count(k + 1) - 1))], v_ssem.at[k])
        drain(ubuf.at[k + 1, pl.ds(8, piece * (u_count(k + 1) - 1))], u_ssem.at[k])
    for out in outs:
        out.wait()


def store(u_ref, v_ref, s_ref, uo_ref, vo_ref, so_ref, s, u, v, in_sems, out_sems):
    order = [(s_ref, s, so_ref), (u_ref, u, uo_ref), (v_ref, v, vo_ref)]
    loads = [pltpu.make_async_copy(a, b, in_sems.at[i]) for i, (a, b, _) in enumerate(order)]
    stores = [pltpu.make_async_copy(b, c, out_sems.at[i]) for i, (_, b, c) in enumerate(order)]
    for load in loads:
        load.start()
    for load, out in zip(loads, stores):
        load.wait()
        out.start()
    for out in stores:
        out.wait()


def shards(group, spectra, scores, loadings, smooth, thresholds, across, down):
    rows, cols, bins = spectra.shape
    rank = loadings.shape[1]
    n_pix, n_mz = lax.axis_size("pix"), lax.axis_size("mz")
    nq = rows * cols // 2
    half = nq // 2
    piece = nq // n_mz
    edge = max(piece // rows, 8)
    srows = rank // group
    n_z, n_team = n_pix // group, 2 * group
    hbm = pl.BlockSpec(memory_space=pltpu.HBM)
    anywhere = pl.BlockSpec(memory_space=pl.ANY)
    dma = pltpu.SemaphoreType.DMA
    vmem = pltpu.VMEM
    args = (
        spectra, scores, loadings.T, smooth.reshape(1, rank), thresholds.reshape(1, bins),
        across, down,
    )
    out_shape = (
        jax.ShapeDtypeStruct(scores.shape, F32),
        jax.ShapeDtypeStruct((rank, bins), F32),
        jax.ShapeDtypeStruct(spectra.shape, BF16),
    )
    outs = pl.pallas_call(
        functools.partial(kernel, group),
        out_shape=out_shape,
        in_specs=[hbm] * 7,
        out_specs=(anywhere,) * 3,
        scratch_shapes=[
            vmem(spectra.shape, BF16),
            vmem(scores.shape, F32),
            vmem((rank, bins), F32),
            vmem((1, rank), F32),
            vmem((1, bins), F32),
            vmem(across.shape, jnp.int32),
            vmem(down.shape, jnp.int32),
            vmem(down.shape, jnp.int32),
            vmem((rows * cols, bins), F32),
            vmem((2, nq, bins), F32),
            vmem((2, half, bins), F32),
            vmem((2, nq, bins), F32),
            vmem((2, half, bins), F32),
            vmem((nq, 256), BF16),
            vmem((nq, 2 * bins), BF16),
            vmem((nq, 2 * bins), BF16),
            vmem((2, 256, 2 * bins), BF16),
            vmem((2, 256, 2 * bins), BF16),
            vmem((ITERS + 1, nq + 16, 128), F32),
            vmem((ITERS + 1, 2, rank, bins), F32),
            vmem((1, bins), F32),
            vmem((ITERS, n_mz, piece + 1, 128), F32),
            vmem((ITERS, n_mz, piece + 1, 128), F32),
            vmem((ITERS, n_team, srows + 8, 128), F32),
            vmem((ITERS, n_team, srows + 8, 128), F32),
            vmem((ITERS, n_z, srows + 8, 128), F32),
            vmem((ITERS, 4, edge, 128), F32),
            vmem((ITERS, 4, edge, 128), F32),
            vmem((piece, cols), F32),
            vmem((2, piece, 128), F32),
            vmem((4, piece, 128), F32),
            dma((7,)),
            dma((3,)),
        ]
        + [dma((ITERS,))] * 10
        + [dma((ITERS, 4))] * 2
        + [dma] * 4
        + [dma((2,))] * 4
        + [dma],
        compiler_params=pltpu.CompilerParams(
            collective_id=0, has_side_effects=True, vmem_limit_bytes=63 * 1024 * 1024
        ),
        cost_estimate=pl.CostEstimate(
            flops=2 * 10 * rows * cols * bins * rank * 3,
            bytes_accessed=2 * (spectra.size * 2 + scores.size * 4),
            transcendentals=0,
        ),
    )(*args)
    score_maps, final, sparse = pl.pallas_call(
        store,
        out_shape=out_shape,
        in_specs=[hbm] * 3,
        out_specs=(hbm,) * 3,
        scratch_shapes=[
            vmem(spectra.shape, BF16),
            vmem(scores.shape, F32),
            vmem((rank, bins), F32),
            dma((3,)),
            dma((3,)),
        ],
        compiler_params=pltpu.CompilerParams(vmem_limit_bytes=63 * 1024 * 1024),
    )(*outs)
    return score_maps, final.T, sparse


def solution(mesh, group=GROUP):
    in_specs = (
        P("pix", None, "mz"),
        P("pix", None),
        P("mz", None),
        P(),
        P("mz"),
        P("pix", None),
        P("pix", None),
    )
    out_specs = (P("pix", None), P("mz", None), P("pix", None, "mz"))
    return jax.shard_map(
        functools.partial(shards, group), mesh=mesh, in_specs=in_specs, out_specs=out_specs,
        check_vma=False,
    )
```

```python
import functools
import jax
import jax.numpy as jnp
from jax import lax
from jax.experimental import pallas as pl
from jax.experimental.pallas import tpu as pltpu
from jax.sharding import PartitionSpec as P

ITERS = 3
GROUP = 8
MESH = pl.DeviceIdType.MESH
F32 = jnp.float32
BF16 = jnp.bfloat16
NT = (((1,), (1,)), ((), ()))
TN = (((0,), (0,)), ((), ()))


def mm(a, b, dims=(((1,), (0,)), ((), ()))):
    return lax.dot_general(a, b, dims, preferred_element_type=F32)


def split(a):
    high = a.astype(BF16)
    return high, (a - high.astype(F32)).astype(BF16)


def kernel(
    group,
    x_hbm, u_hbm, v_hbm, smooth_hbm, thr_hbm, across_hbm, down_hbm,
    uo_ref, vo_ref, so_ref,
    x_in, u_in, v_in, smooth_in, thr_in, across_in, down_in, down_above,
    xf, x_own, x_other, c_own, c_other, u_hl, d_h, d_l, b_hh, b_hl, ubuf, vbuf, thr_other,
    g_send, g_recv, h_send, h_recv, z_recv, halo_send, halo_recv,
    wtmp, shift, weights,
    in_sems, out_sems, g_ssem, g_rsem, u_ssem, u_rsem, h_ssem, h_rsem, z_ssem, z_rsem,
    v_ssem, v_rsem, halo_ssem, halo_rsem, down_ssem, down_rsem, thr_ssem, thr_rsem,
    x_ssem, x_rsem, c_ssem, c_rsem, cross_rsem, first_ssem, first_rsem,
):
    n_pix, n_mz = lax.axis_size("pix"), lax.axis_size("mz")
    pix, mz = lax.axis_index("pix"), lax.axis_index("mz")
    n_z, n_y = 2 * (n_pix // group), n_mz // 2
    block, spot = pix // group, pix % group
    y, side = mz // 2, mz % 2
    strip, zed = side * n_y + y, 2 * block + side
    twin = (pix, 2 * y + 1 - side)
    rows, cols, bins = x_in.shape
    rank = v_in.shape[0]
    nq = rows * cols // 2
    half = nq // 2
    piece = nq // n_mz
    pairs = piece // rows
    srows = rank // group
    below, above = (pix + 1) % n_pix, (pix + n_pix - 1) % n_pix

    barrier = pltpu.get_barrier_semaphore()

    def greet(device):
        pl.semaphore_signal(barrier, inc=1, device_id=device, device_id_type=MESH)

    def each(count, act):
        lax.fori_loop(0, count, lambda i, _: (act(i), 0)[1], 0)

    def far_first(at, i, n):
        return (at + n // 2 + ((i + 1) // 2) * (1 - 2 * (i % 2)) + n) % n

    def y_peer(i):
        return far_first(y, i, n_y)

    def mz_peer(i):
        return 2 * y_peer(i // 2) + (side + 1 - i % 2) % 2

    def group_device(i):
        return (block * group + far_first(spot, i, group), mz)

    def z_device(i):
        to = far_first(zed, i, n_z)
        return (to // 2 * group + spot, 2 * y + to % 2)

    def strip_device(j):
        return (pix, 2 * (j % n_y) + j // n_y)

    loads = [
        pltpu.make_async_copy(src, dst, in_sems.at[i])
        for i, (src, dst) in enumerate(
            [
                (u_hbm, u_in), (v_hbm, v_in), (x_hbm, x_in), (thr_hbm, thr_in),
                (down_hbm, down_in), (across_hbm, across_in), (smooth_hbm, smooth_in),
            ]
        )
    ]
    for load in loads:
        load.start()

    each(n_mz - 1, lambda i: greet((pix, mz_peer(i))))
    each(group - 1, lambda i: greet(group_device(i)))
    each(n_z - 1, lambda i: greet(z_device(i)))
    greet((below, mz))
    greet((above, mz))

    def remote(src, dst, ssem, rsem, device):
        return pltpu.make_async_remote_copy(
            src_ref=src, dst_ref=dst, send_sem=ssem, recv_sem=rsem,
            device_id=device, device_id_type=MESH,
        )

    def drain(ref, sem):
        pltpu.make_async_copy(ref, ref, sem).wait()

    def my_rows():
        return pl.ds(pl.multiple_of(8 + piece * strip, 8), piece)

    def half_rows(which, at=0, count=half):
        return pl.ds(pl.multiple_of(half * which + at, 8), count)

    zeros8 = jnp.zeros((8, 128), F32)
    ubuf[0, 0:8, :] = zeros8
    ubuf[0, 8 + nq : 16 + nq, :] = zeros8
    b_hh[...] = jnp.zeros_like(b_hh)
    b_hl[...] = jnp.zeros_like(b_hl)
    for load in loads[:4]:
        load.wait()
    for t in range(cols // 2):
        ubuf[0, 8 + rows * t : 8 + rows * (t + 1), :] = u_in[:, 128 * t : 128 * (t + 1)]
    vbuf[0, side] = v_in[...]
    xf[...] = x_in[...].reshape(rows * cols, bins).astype(F32)
    for r in range(rows):
        for par in range(2):
            x_own[par, pl.ds(r, cols // 2, stride=rows), :] = xf[
                pl.ds(r * cols + par, cols // 2, stride=2), :
            ]

    def halos(k):
        to = ((above, mz), (below, mz), strip_device((strip + n_mz - 1) % n_mz),
              strip_device((strip + 1) % n_mz))
        return [
            remote(
                halo_send.at[k, i], halo_recv.at[k, i ^ 1], halo_ssem.at[k, i],
                halo_rsem.at[k, i ^ 1], to[i],
            )
            for i in range(2 if k == 0 else 4)
        ]

    def send_halos(k, mine):
        shift[0] = mine
        halo_send[k, 0, 0:pairs, :] = shift[0, pl.ds(0, pairs, stride=rows), :]
        halo_send[k, 1, 0:pairs, :] = shift[0, pl.ds(rows - 1, pairs, stride=rows), :]
        halo_send[k, 2, 0:8, :] = mine[0:8]
        halo_send[k, 3, 0:8, :] = mine[piece - 8 : piece]
        for copy in halos(k):
            copy.start()

    chunk = 128

    def factors(k, slot):
        high, low = split(vbuf[k, side if slot == 0 else 1 - side])
        for at, part in ((0, high), (128, high)):
            b_hh[slot, at : at + rank, 0:bins] = part
            b_hh[slot, at + rank : at + 2 * rank, bins : 2 * bins] = part
        for at, part in ((0, high), (128, low)):
            b_hl[slot, at : at + rank, 0:bins] = part
            b_hl[slot, at + rank : at + 2 * rank, bins : 2 * bins] = part

    def sweep(k, which=None):
        paired = 0 < k < ITERS
        slots = (0, 1) if paired else (0,)
        vsq = jnp.zeros((1, 128), F32)
        for slot in slots if which is None or which is side else ():
            factors(k, slot)
            v = vbuf[k, side if slot == 0 else 1 - side]
            vsq = vsq + jnp.sum(v * v, axis=0, keepdims=True)
        usq = zeros8
        for q in range(0, nq if k == 0 else half, chunk):
            here = pl.ds(q, chunk)
            own = here if k == 0 else half_rows(side if which is None else which, q, chunk)
            u = ubuf[k, pl.ds(pl.multiple_of(own.start + 8, 8), chunk), :]
            u_h, u_l = split(u)
            u_hl[here, 0:128] = u_h
            u_hl[here, 128:256] = u_l
            usq = usq + jnp.sum((u * u).reshape(chunk // 8, 8, 128), axis=0)
            g = None
            for slot in slots:
                approx = mm(u_hl[here, :], b_hh[slot]) + mm(u_h, b_hl[slot, 128:256, :])
                thr = (thr_other if slot else thr_in)[...]
                x, c = (x_other, c_other) if slot else (x_own, c_own)
                spot_rows = here if slot else own
                dest = pl.ds(slot * half + q, chunk)
                for par in range(2):
                    lanes = slice(par * bins, (par + 1) * bins)
                    low = approx[:, lanes]
                    data = x[par, spot_rows, :]
                    if k == 0:
                        d = low - data
                    else:
                        t = data - low
                        if k > 1:
                            old = c[par, spot_rows, :]
                            t = t + old
                        clipped = jnp.clip(t, -thr, thr)
                        if k == ITERS:
                            c[par, spot_rows, :] = t - clipped
                            continue
                        c[par, spot_rows, :] = clipped
                        d = -2.0 * clipped
                        if k > 1:
                            d = d + old
                    high, low = split(d)
                    d_h[dest, lanes] = high
                    d_l[dest, lanes] = low
                if k == ITERS:
                    continue
                g2 = mm(d_h[dest, :], b_hl[slot], NT)
                part = g2[:, 0:128] + g2[:, 128:256] + mm(d_l[dest, :], b_hh[slot, 0:128, :], NT)
                g = part if g is None else g + part
            if k == ITERS:
                continue
            for j in range(q // piece, (q + chunk) // piece):
                g_send[k, j, 0:piece, :] = g[j * piece - q : (j + 1) * piece - q, :]
                g_send[k, j, piece : piece + 1, :] = vsq
        return usq

    def send_g(k, i):
        if k == 0:
            to = mz_peer(i)
            return remote(
                g_send.at[k, (to % 2) * n_y + to // 2], g_recv.at[k, mz], g_ssem.at[k],
                g_rsem.at[k], (pix, to),
            )
        to = y_peer(i)
        return remote(
            g_send.at[k, to], g_recv.at[k, y], g_ssem.at[k], g_rsem.at[k], (pix, 2 * to + side)
        )

    def send_h(k, i):
        return remote(
            h_send.at[k, far_first(spot, i, group)], h_recv.at[k, spot], h_ssem.at[k],
            h_rsem.at[k], group_device(i),
        )

    def send_z(k, i):
        ref = z_recv.at[k, zed]
        return remote(ref, ref, z_ssem.at[k], z_rsem.at[k], z_device(i))

    def v_rows():
        return pl.ds(pl.multiple_of(srows * spot, 8), srows)

    def send_v(k, i):
        ref = vbuf.at[k, pl.ds(0, 2), v_rows()]
        return remote(ref, ref, v_ssem.at[k - 1], v_rsem.at[k - 1], group_device(i))

    def send_u(k, to, rsem=None):
        ref = ubuf.at[k, my_rows()]
        rsem = u_rsem.at[k - 1] if rsem is None else rsem
        return remote(ref, ref, u_ssem.at[k - 1], rsem, (pix, to))

    def g_count(k):
        return n_mz if k == 0 else n_y

    def u_count(k):
        return n_mz if k == ITERS else n_y

    def start_g(k):
        each(g_count(k) - 1, lambda i: send_g(k, i).start())

    def h_part(k, usq):
        for slot in (0,) if k == 0 else (0, 1):
            n = nq if k == 0 else half
            dest = slice(slot * half, slot * half + n)
            both = mm(u_hl[0:n, :], d_h[dest, :], TN)
            prod = both[0:128, :] + both[128:256, :] + mm(u_hl[0:n, 0:128], d_l[dest, :], TN)
            h = prod[0:rank, 0:bins] + prod[rank : 2 * rank, bins : 2 * bins]
            at = srows * (side if slot == 0 else 1 - side)
            for j in range(group):
                h_send[k, j, pl.ds(pl.multiple_of(at, 8), srows), :] = h[
                    j * srows : (j + 1) * srows, :
                ]
        usq = jnp.sum(usq, axis=0, keepdims=True)
        if k == 0:
            usq = 0.5 * usq
            at = pl.ds(pl.multiple_of(srows * (1 - side), 8), srows)
            for j in range(group):
                h_send[k, j, at, :] = jnp.zeros((srows, 128), F32)
        for j in range(group):
            h_send[k, j, 2 * srows : 2 * srows + 1, :] = usq
        each(group - 1, lambda i: send_h(k, i).start())

    usq = sweep(0)
    pl.semaphore_wait(barrier, n_mz - 1 + group - 1 + n_z - 1 + 2)
    x_copies = [
        remote(
            x_own.at[par, half_rows(1 - side)], x_other.at[par], x_ssem.at[par], x_rsem.at[par],
            twin,
        )
        for par in range(2)
    ]
    start_g(0)
    h_part(0, usq)
    send_halos(0, ubuf[0, my_rows(), :])
    thr_copy = remote(thr_in, thr_other, thr_ssem, thr_rsem, twin)
    thr_copy.start()
    v_ref = vbuf.at[0, side]
    v_copy = remote(v_ref, v_ref, first_ssem, first_rsem, twin)
    v_copy.start()
    loads[4].wait()
    down_copy = remote(down_in, down_above, down_ssem, down_rsem, (below, mz))
    down_copy.start()
    c_copies = [
        remote(
            c_other.at[par], c_own.at[par, half_rows(side)], c_ssem.at[par], c_rsem.at[par],
            twin,
        )
        for par in range(2)
    ]

    for load in loads[5:]:
        load.wait()
    q_col = lax.broadcasted_iota(jnp.int32, (piece, cols), 0) // rows + pairs * strip
    q_row = lax.broadcasted_iota(jnp.int32, (piece, cols), 0) % rows
    col = lax.broadcasted_iota(jnp.int32, (piece, cols), 1)
    p_col = lax.broadcasted_iota(jnp.int32, (cols, 128), 0)
    p_half = lax.broadcasted_iota(jnp.int32, (cols, 128), 1) // 64

    def spread(which, keep, offset):
        pick = jnp.where(keep & ((col + offset) // 2 == q_col), wtmp[...], 0.0)
        place = jnp.where((p_col + offset) % 2 == p_half, 0.25, 0.0)
        weights[which] = mm(pick.astype(BF16), place.astype(BF16))

    levels = across_in[...].astype(F32) + 1.0
    for t in range(pairs):
        wtmp[rows * t : rows * (t + 1), :] = levels
    spread(0, col < cols - 1, 0)
    spread(1, col < cols - 1, 1)
    levels = down_in[...].astype(F32) + 1.0
    for t in range(pairs):
        wtmp[rows * t : rows * (t + 1), :] = levels
    spread(2, (q_row < rows - 1) | (pix < n_pix - 1), 0)
    down_copy.wait()
    for t in range(pairs):
        wtmp[rows * t : rows * t + 1, :] = down_above[rows - 1 : rows, :].astype(F32) + 1.0
        wtmp[rows * t + 1 : rows * (t + 1), :] = levels[0 : rows - 1, :]
    spread(3, (q_row > 0) | (pix > 0), 0)

    smooth = jnp.concatenate([smooth_in[...], smooth_in[...]], axis=1)
    lane = lax.broadcasted_iota(jnp.int32, (piece, 128), 1)

    def laplace(k):
        for copy in halos(k):
            copy.wait()
        if k == 0:
            window = ubuf[k, pl.ds(pl.multiple_of(piece * strip, 8), piece + 16), :]
        else:
            window = jnp.concatenate(
                [halo_recv[k, 2, 0:8, :], ubuf[k, my_rows(), :], halo_recv[k, 3, 0:8, :]], axis=0
            )
        mine = window[8 : 8 + piece]
        swapped = pltpu.roll(mine, 64, 1)
        before = pltpu.roll(window[8 - rows : 8 - rows + piece], 64, 1)
        after = pltpu.roll(window[8 + rows : 8 + rows + piece], 64, 1)
        right = jnp.where(lane < 64, swapped, after)
        left = jnp.where(lane < 64, before, swapped)
        shift[0] = window[7 : 7 + piece]
        shift[1] = window[9 : 9 + piece]
        shift[0, pl.ds(0, pairs, stride=rows), :] = halo_recv[k, 0, 0:pairs, :]
        shift[1, pl.ds(rows - 1, pairs, stride=rows), :] = halo_recv[k, 1, 0:pairs, :]
        flow = weights[0] * (mine - right) + weights[1] * (mine - left)
        flow = flow + weights[2] * (mine - shift[1]) + weights[3] * (mine - shift[0])
        return mine, flow * smooth

    for k in range(ITERS):
        mine, lap = laplace(k)
        drain(h_recv.at[k, pl.ds(0, group - 1)], h_rsem.at[k])
        h_recv[k, spot] = h_send[k, spot]
        total = h_recv[k, 0]
        for j in range(1, group):
            total = total + h_recv[k, j]
        z_recv[k, zed] = total
        each(n_z - 1, lambda i: send_z(k, i).start())
        if k == 0:
            x_copies[0].start()
        if k == ITERS - 1:
            c_copies[1].start()
        drain(g_recv.at[k, pl.ds(0, g_count(k) - 1)], g_rsem.at[k])
        if k == 0:
            g_recv[k, mz] = g_send[k, strip]
        else:
            g_recv[k, y] = g_send[k, y]
        total = g_recv[k, 0]
        for j in range(1, g_count(k)):
            total = total + g_recv[k, j]
        vsq = jnp.sum(total[piece:, :])
        eta_u = 1.0 / (jnp.full((1, 128), vsq, F32) / rank + 8.0 * smooth + 1.0)
        mine = mine - eta_u * (total[0:piece, :] + lap)
        ubuf[k + 1, my_rows(), :] = mine
        if k + 1 < ITERS:
            each(n_y - 1, lambda i: send_u(k + 1, 2 * y_peer(i) + side).start())
            send_halos(k + 1, mine)
            if k == 0:
                x_copies[1].start()
        else:
            def both_sides(i):
                send_u(k + 1, 2 * y_peer(i) + 1 - side, cross_rsem).start()
                send_u(k + 1, 2 * y_peer(i) + side).start()

            each(n_y - 1, both_sides)
            send_u(k + 1, 2 * y + 1 - side, cross_rsem).start()
        drain(z_recv.at[k, pl.ds(0, n_z - 1)], z_rsem.at[k])
        total = z_recv[k, 0]
        for j in range(1, n_z):
            total = total + z_recv[k, j]
        usq = jnp.sum(total[2 * srows :, :])
        eta_v = 1.0 / (jnp.full((1, 128), usq, F32) / rank + 1.0)
        if k == 0:
            v_copy.wait()
        for b in range(2):
            vbuf[k + 1, b, v_rows(), :] = (
                vbuf[k, b, v_rows(), :] - eta_v * total[b * srows : (b + 1) * srows, :]
            )
        each(group - 1, lambda i: send_v(k + 1, i).start())
        if k == 0:
            thr_copy.wait()
            for copy in x_copies:
                copy.wait()
        drain(ubuf.at[0, pl.ds(0, 2 * srows * (group - 1))], v_rsem.at[k])
        drain(ubuf.at[k + 1, pl.ds(8, piece * (n_y - 1))], u_rsem.at[k])
        if k + 1 < ITERS:
            usq = sweep(k + 1)
            start_g(k + 1)
            h_part(k + 1, usq)
            if k + 2 == ITERS:
                c_copies[0].start()

    sweep(ITERS, side)
    v_in[...] = vbuf[ITERS, side]
    outs = [
        pltpu.make_async_copy(src, dst, out_sems.at[i])
        for i, (src, dst) in enumerate([(u_in, uo_ref), (v_in, vo_ref), (x_in, so_ref)])
    ]
    outs[1].start()
    drain(ubuf.at[ITERS, pl.ds(8, piece * n_y)], cross_rsem)
    for copy in c_copies:
        copy.wait()
    for t in range(cols // 2):
        u_in[:, 128 * t : 128 * (t + 1)] = ubuf[ITERS, 8 + rows * t : 8 + rows * (t + 1), :]
    outs[0].start()
    sweep(ITERS, 1 - side)
    for r in range(rows):
        for par in range(2):
            xf[pl.ds(r * cols + par, cols // 2, stride=2), :] = c_own[
                par, pl.ds(r, cols // 2, stride=rows), :
            ]
    x_in[...] = xf[...].astype(BF16).reshape(rows, cols, bins)
    outs[2].start()

    for k in range(ITERS):
        drain(g_send.at[k, pl.ds(0, g_count(k) - 1)], g_ssem.at[k])
        drain(h_send.at[k, pl.ds(0, group - 1)], h_ssem.at[k])
        drain(z_recv.at[k, pl.ds(0, n_z - 1)], z_ssem.at[k])
        drain(ubuf.at[0, pl.ds(0, 2 * srows * (group - 1))], v_ssem.at[k])
        drain(ubuf.at[k + 1, pl.ds(8, piece * (u_count(k + 1) - 1))], u_ssem.at[k])
    for out in outs:
        out.wait()


def store(u_ref, v_ref, s_ref, uo_ref, vo_ref, so_ref, s, u, v, in_sems, out_sems):
    order = [(s_ref, s, so_ref), (u_ref, u, uo_ref), (v_ref, v, vo_ref)]
    loads = [pltpu.make_async_copy(a, b, in_sems.at[i]) for i, (a, b, _) in enumerate(order)]
    stores = [pltpu.make_async_copy(b, c, out_sems.at[i]) for i, (_, b, c) in enumerate(order)]
    for load in loads:
        load.start()
    for load, out in zip(loads, stores):
        load.wait()
        out.start()
    for out in stores:
        out.wait()


def shards(group, spectra, scores, loadings, smooth, thresholds, across, down):
    rows, cols, bins = spectra.shape
    rank = loadings.shape[1]
    n_pix, n_mz = lax.axis_size("pix"), lax.axis_size("mz")
    nq = rows * cols // 2
    half = nq // 2
    piece = nq // n_mz
    edge = max(piece // rows, 8)
    srows = rank // group
    n_z = 2 * (n_pix // group)
    hbm = pl.BlockSpec(memory_space=pltpu.HBM)
    anywhere = pl.BlockSpec(memory_space=pl.ANY)
    dma = pltpu.SemaphoreType.DMA
    vmem = pltpu.VMEM
    args = (
        spectra, scores, loadings.T, smooth.reshape(1, rank), thresholds.reshape(1, bins),
        across, down,
    )
    out_shape = (
        jax.ShapeDtypeStruct(scores.shape, F32),
        jax.ShapeDtypeStruct((rank, bins), F32),
        jax.ShapeDtypeStruct(spectra.shape, BF16),
    )
    outs = pl.pallas_call(
        functools.partial(kernel, group),
        out_shape=out_shape,
        in_specs=[hbm] * 7,
        out_specs=(anywhere,) * 3,
        scratch_shapes=[
            vmem(spectra.shape, BF16),
            vmem(scores.shape, F32),
            vmem((rank, bins), F32),
            vmem((1, rank), F32),
            vmem((1, bins), F32),
            vmem(across.shape, jnp.int32),
            vmem(down.shape, jnp.int32),
            vmem(down.shape, jnp.int32),
            vmem((rows * cols, bins), F32),
            vmem((2, nq, bins), F32),
            vmem((2, half, bins), F32),
            vmem((2, nq, bins), F32),
            vmem((2, half, bins), F32),
            vmem((nq, 256), BF16),
            vmem((nq, 2 * bins), BF16),
            vmem((nq, 2 * bins), BF16),
            vmem((2, 256, 2 * bins), BF16),
            vmem((2, 256, 2 * bins), BF16),
            vmem((ITERS + 1, nq + 16, 128), F32),
            vmem((ITERS + 1, 2, rank, bins), F32),
            vmem((1, bins), F32),
            vmem((ITERS, n_mz, piece + 1, 128), F32),
            vmem((ITERS, n_mz, piece + 1, 128), F32),
            vmem((ITERS, group, 2 * srows + 1, 128), F32),
            vmem((ITERS, group, 2 * srows + 1, 128), F32),
            vmem((ITERS, n_z, 2 * srows + 1, 128), F32),
            vmem((ITERS, 4, edge, 128), F32),
            vmem((ITERS, 4, edge, 128), F32),
            vmem((piece, cols), F32),
            vmem((2, piece, 128), F32),
            vmem((4, piece, 128), F32),
            dma((7,)),
            dma((3,)),
        ]
        + [dma((ITERS,))] * 10
        + [dma((ITERS, 4))] * 2
        + [dma] * 4
        + [dma((2,))] * 4
        + [dma] * 3,
        compiler_params=pltpu.CompilerParams(
            collective_id=0, has_side_effects=True, vmem_limit_bytes=63 * 1024 * 1024
        ),
        cost_estimate=pl.CostEstimate(
            flops=2 * 10 * rows * cols * bins * rank * 3,
            bytes_accessed=2 * (spectra.size * 2 + scores.size * 4),
            transcendentals=0,
        ),
    )(*args)
    score_maps, final, sparse = pl.pallas_call(
        store,
        out_shape=out_shape,
        in_specs=[hbm] * 3,
        out_specs=(hbm,) * 3,
        scratch_shapes=[
            vmem(spectra.shape, BF16),
            vmem(scores.shape, F32),
            vmem((rank, bins), F32),
            dma((3,)),
            dma((3,)),
        ],
        compiler_params=pltpu.CompilerParams(vmem_limit_bytes=63 * 1024 * 1024),
    )(*outs)
    return score_maps, final.T, sparse


def solution(mesh, group=GROUP):
    in_specs = (
        P("pix", None, "mz"),
        P("pix", None),
        P("mz", None),
        P(),
        P("mz"),
        P("pix", None),
        P("pix", None),
    )
    out_specs = (P("pix", None), P("mz", None), P("pix", None, "mz"))
    return jax.shard_map(
        functools.partial(shards, group), mesh=mesh, in_specs=in_specs, out_specs=out_specs,
        check_vma=False,
    )
```

```python
import functools
import jax
import jax.numpy as jnp
from jax import lax
from jax.experimental import pallas as pl
from jax.experimental.pallas import tpu as pltpu
from jax.sharding import PartitionSpec as P

ITERS = 3
GROUP = 8
MESH = pl.DeviceIdType.MESH
F32 = jnp.float32
BF16 = jnp.bfloat16
NT = (((1,), (1,)), ((), ()))
TN = (((0,), (0,)), ((), ()))


def mm(a, b, dims=(((1,), (0,)), ((), ()))):
    return lax.dot_general(a, b, dims, preferred_element_type=F32)


def split(a):
    high = a.astype(BF16)
    return high, (a - high.astype(F32)).astype(BF16)


def kernel(
    group,
    x_hbm, u_hbm, v_hbm, smooth_hbm, thr_hbm, across_hbm, down_hbm,
    uo_ref, vo_ref, so_ref,
    x_in, u_in, v_in, smooth_in, thr_in, across_in, down_in, down_above,
    xf, x_own, x_other, c_own, c_other, u_hl, d_h, d_l, b_hh, b_hl, ubuf, vbuf, thr_other,
    g_send, g_recv, h_send, h_recv, z_recv, halo_send, halo_recv,
    wtmp, shift, weights,
    in_sems, out_sems, g_ssem, g_rsem, u_ssem, u_rsem, h_ssem, h_rsem, z_ssem, z_rsem,
    v_ssem, v_rsem, halo_ssem, halo_rsem, down_ssem, down_rsem, thr_ssem, thr_rsem,
    x_ssem, x_rsem, c_ssem, c_rsem, cross_rsem, first_ssem, first_rsem,
):
    n_pix, n_mz = lax.axis_size("pix"), lax.axis_size("mz")
    pix, mz = lax.axis_index("pix"), lax.axis_index("mz")
    n_z, n_y = 2 * (n_pix // group), n_mz // 2
    block, spot = pix // group, pix % group
    y, side = mz // 2, mz % 2
    strip, zed = side * n_y + y, 2 * block + side
    twin = (pix, 2 * y + 1 - side)
    rows, cols, bins = x_in.shape
    rank = v_in.shape[0]
    nq = rows * cols // 2
    half = nq // 2
    piece = nq // n_mz
    pairs = piece // rows
    srows = rank // group
    below, above = (pix + 1) % n_pix, (pix + n_pix - 1) % n_pix

    barrier = pltpu.get_barrier_semaphore()

    def greet(device):
        pl.semaphore_signal(barrier, inc=1, device_id=device, device_id_type=MESH)

    def each(count, act):
        lax.fori_loop(0, count, lambda i, _: (act(i), 0)[1], 0)

    def far_first(at, i, n):
        return (at + n // 2 + ((i + 1) // 2) * (1 - 2 * (i % 2)) + n) % n

    def y_peer(i):
        return far_first(y, i, n_y)

    def mz_peer(i):
        return 2 * y_peer(i // 2) + (side + 1 - i % 2) % 2

    def group_device(i):
        return (block * group + far_first(spot, i, group), mz)

    def z_device(i):
        to = far_first(zed, i, n_z)
        return (to // 2 * group + spot, 2 * y + to % 2)

    def strip_device(j):
        return (pix, 2 * (j % n_y) + j // n_y)

    loads = [
        pltpu.make_async_copy(src, dst, in_sems.at[i])
        for i, (src, dst) in enumerate(
            [
                (u_hbm, u_in), (v_hbm, v_in), (x_hbm, x_in), (thr_hbm, thr_in),
                (down_hbm, down_in), (across_hbm, across_in), (smooth_hbm, smooth_in),
            ]
        )
    ]
    for load in loads:
        load.start()

    each(n_mz - 1, lambda i: greet((pix, mz_peer(i))))
    each(group - 1, lambda i: greet(group_device(i)))
    each(n_z - 1, lambda i: greet(z_device(i)))
    greet((below, mz))
    greet((above, mz))

    def remote(src, dst, ssem, rsem, device):
        return pltpu.make_async_remote_copy(
            src_ref=src, dst_ref=dst, send_sem=ssem, recv_sem=rsem,
            device_id=device, device_id_type=MESH,
        )

    def drain(ref, sem):
        pltpu.make_async_copy(ref, ref, sem).wait()

    def my_rows():
        return pl.ds(pl.multiple_of(8 + piece * strip, 8), piece)

    def half_rows(which, at=0, count=half):
        return pl.ds(pl.multiple_of(half * which + at, 8), count)

    zeros8 = jnp.zeros((8, 128), F32)
    ubuf[0, 0:8, :] = zeros8
    ubuf[0, 8 + nq : 16 + nq, :] = zeros8
    b_hh[...] = jnp.zeros_like(b_hh)
    b_hl[...] = jnp.zeros_like(b_hl)
    for load in loads[:4]:
        load.wait()
    for t in range(cols // 2):
        ubuf[0, 8 + rows * t : 8 + rows * (t + 1), :] = u_in[:, 128 * t : 128 * (t + 1)]
    vbuf[0, side] = v_in[...]
    xf[...] = x_in[...].reshape(rows * cols, bins).astype(F32)
    for r in range(rows):
        for par in range(2):
            x_own[par, pl.ds(r, cols // 2, stride=rows), :] = xf[
                pl.ds(r * cols + par, cols // 2, stride=2), :
            ]

    def halos(k):
        to = ((above, mz), (below, mz), strip_device((strip + n_mz - 1) % n_mz),
              strip_device((strip + 1) % n_mz))
        return [
            remote(
                halo_send.at[k, i], halo_recv.at[k, i ^ 1], halo_ssem.at[k, i],
                halo_rsem.at[k, i ^ 1], to[i],
            )
            for i in range(2 if k == 0 else 4)
        ]

    def send_halos(k, mine):
        shift[0] = mine
        halo_send[k, 0, 0:pairs, :] = shift[0, pl.ds(0, pairs, stride=rows), :]
        halo_send[k, 1, 0:pairs, :] = shift[0, pl.ds(rows - 1, pairs, stride=rows), :]
        halo_send[k, 2, 0:8, :] = mine[0:8]
        halo_send[k, 3, 0:8, :] = mine[piece - 8 : piece]
        for copy in halos(k):
            copy.start()

    chunk = 128

    def factors(k, slot):
        high, low = split(vbuf[k, side if slot == 0 else 1 - side])
        for at, part in ((0, high), (128, high)):
            b_hh[slot, at : at + rank, 0:bins] = part
            b_hh[slot, at + rank : at + 2 * rank, bins : 2 * bins] = part
        for at, part in ((0, high), (128, low)):
            b_hl[slot, at : at + rank, 0:bins] = part
            b_hl[slot, at + rank : at + 2 * rank, bins : 2 * bins] = part

    def sweep(k, which=None):
        paired = 0 < k < ITERS
        slots = (0, 1) if paired else (0,)
        vsq = jnp.zeros((1, 128), F32)
        for slot in slots if which is None or which is side else ():
            factors(k, slot)
            v = vbuf[k, side if slot == 0 else 1 - side]
            vsq = vsq + jnp.sum(v * v, axis=0, keepdims=True)
        usq = zeros8
        for q in range(0, nq if k == 0 else half, chunk):
            here = pl.ds(q, chunk)
            own = here if k == 0 else half_rows(side if which is None else which, q, chunk)
            u = ubuf[k, pl.ds(pl.multiple_of(own.start + 8, 8), chunk), :]
            u_h, u_l = split(u)
            u_hl[here, 0:128] = u_h
            u_hl[here, 128:256] = u_l
            usq = usq + jnp.sum((u * u).reshape(chunk // 8, 8, 128), axis=0)
            g = None
            for slot in slots:
                approx = mm(u_hl[here, :], b_hh[slot]) + mm(u_h, b_hl[slot, 128:256, :])
                thr = (thr_other if slot else thr_in)[...]
                x, c = (x_other, c_other) if slot else (x_own, c_own)
                spot_rows = here if slot else own
                dest = pl.ds(slot * half + q, chunk)
                for par in range(2):
                    lanes = slice(par * bins, (par + 1) * bins)
                    low = approx[:, lanes]
                    data = x[par, spot_rows, :]
                    if k == 0:
                        d = low - data
                    else:
                        t = data - low
                        if k > 1:
                            old = c[par, spot_rows, :]
                            t = t + old
                        clipped = jnp.clip(t, -thr, thr)
                        if k == ITERS:
                            x_other[par, here, :] = t - clipped
                            continue
                        c[par, spot_rows, :] = clipped
                        d = -2.0 * clipped
                        if k > 1:
                            d = d + old
                    high, low = split(d)
                    d_h[dest, lanes] = high
                    d_l[dest, lanes] = low
                if k == ITERS:
                    continue
                g2 = mm(d_h[dest, :], b_hl[slot], NT)
                part = g2[:, 0:128] + g2[:, 128:256] + mm(d_l[dest, :], b_hh[slot, 0:128, :], NT)
                g = part if g is None else g + part
            if k == ITERS:
                continue
            for j in range(q // piece, (q + chunk) // piece):
                g_send[k, j, 0:piece, :] = g[j * piece - q : (j + 1) * piece - q, :]
                g_send[k, j, piece : piece + 1, :] = vsq
        return usq

    def send_g(k, i):
        if k == 0:
            to = mz_peer(i)
            return remote(
                g_send.at[k, (to % 2) * n_y + to // 2], g_recv.at[k, mz], g_ssem.at[k],
                g_rsem.at[k], (pix, to),
            )
        to = y_peer(i)
        return remote(
            g_send.at[k, to], g_recv.at[k, y], g_ssem.at[k], g_rsem.at[k], (pix, 2 * to + side)
        )

    def send_h(k, i):
        return remote(
            h_send.at[k, far_first(spot, i, group)], h_recv.at[k, spot], h_ssem.at[k],
            h_rsem.at[k], group_device(i),
        )

    def send_z(k, i):
        ref = z_recv.at[k, zed]
        return remote(ref, ref, z_ssem.at[k], z_rsem.at[k], z_device(i))

    def v_rows():
        return pl.ds(pl.multiple_of(srows * spot, 8), srows)

    def send_v(k, i):
        ref = vbuf.at[k, pl.ds(0, 2), v_rows()]
        return remote(ref, ref, v_ssem.at[k - 1], v_rsem.at[k - 1], group_device(i))

    def send_u(k, to, rsem=None):
        ref = ubuf.at[k, my_rows()]
        rsem = u_rsem.at[k - 1] if rsem is None else rsem
        return remote(ref, ref, u_ssem.at[k - 1], rsem, (pix, to))

    def g_count(k):
        return n_mz if k == 0 else n_y

    def u_count(k):
        return n_mz if k == ITERS else n_y

    def start_g(k):
        each(g_count(k) - 1, lambda i: send_g(k, i).start())

    def h_part(k, usq):
        for slot in (0,) if k == 0 else (0, 1):
            n = nq if k == 0 else half
            dest = slice(slot * half, slot * half + n)
            both = mm(u_hl[0:n, :], d_h[dest, :], TN)
            prod = both[0:128, :] + both[128:256, :] + mm(u_hl[0:n, 0:128], d_l[dest, :], TN)
            h = prod[0:rank, 0:bins] + prod[rank : 2 * rank, bins : 2 * bins]
            at = srows * (side if slot == 0 else 1 - side)
            for j in range(group):
                h_send[k, j, pl.ds(pl.multiple_of(at, 8), srows), :] = h[
                    j * srows : (j + 1) * srows, :
                ]
        usq = jnp.sum(usq, axis=0, keepdims=True)
        if k == 0:
            usq = 0.5 * usq
            at = pl.ds(pl.multiple_of(srows * (1 - side), 8), srows)
            for j in range(group):
                h_send[k, j, at, :] = jnp.zeros((srows, 128), F32)
        for j in range(group):
            h_send[k, j, 2 * srows : 2 * srows + 1, :] = usq
        each(group - 1, lambda i: send_h(k, i).start())

    usq = sweep(0)
    pl.semaphore_wait(barrier, n_mz - 1 + group - 1 + n_z - 1 + 2)
    x_copies = [
        remote(
            x_own.at[par, half_rows(1 - side)], x_other.at[par], x_ssem.at[par], x_rsem.at[par],
            twin,
        )
        for par in range(2)
    ]
    start_g(0)
    h_part(0, usq)
    send_halos(0, ubuf[0, my_rows(), :])
    thr_copy = remote(thr_in, thr_other, thr_ssem, thr_rsem, twin)
    thr_copy.start()
    v_ref = vbuf.at[0, side]
    v_copy = remote(v_ref, v_ref, first_ssem, first_rsem, twin)
    v_copy.start()
    loads[4].wait()
    down_copy = remote(down_in, down_above, down_ssem, down_rsem, (below, mz))
    down_copy.start()
    c_copies = [
        remote(
            c_other.at[par], c_own.at[par, half_rows(side)], c_ssem.at[par], c_rsem.at[par],
            twin,
        )
        for par in range(2)
    ]

    for load in loads[5:]:
        load.wait()
    q_col = lax.broadcasted_iota(jnp.int32, (piece, cols), 0) // rows + pairs * strip
    q_row = lax.broadcasted_iota(jnp.int32, (piece, cols), 0) % rows
    col = lax.broadcasted_iota(jnp.int32, (piece, cols), 1)
    p_col = lax.broadcasted_iota(jnp.int32, (cols, 128), 0)
    p_half = lax.broadcasted_iota(jnp.int32, (cols, 128), 1) // 64

    def spread(which, keep, offset):
        pick = jnp.where(keep & ((col + offset) // 2 == q_col), wtmp[...], 0.0)
        place = jnp.where((p_col + offset) % 2 == p_half, 0.25, 0.0)
        weights[which] = mm(pick.astype(BF16), place.astype(BF16))

    levels = across_in[...].astype(F32) + 1.0
    for t in range(pairs):
        wtmp[rows * t : rows * (t + 1), :] = levels
    spread(0, col < cols - 1, 0)
    spread(1, col < cols - 1, 1)
    levels = down_in[...].astype(F32) + 1.0
    for t in range(pairs):
        wtmp[rows * t : rows * (t + 1), :] = levels
    spread(2, (q_row < rows - 1) | (pix < n_pix - 1), 0)
    down_copy.wait()
    for t in range(pairs):
        wtmp[rows * t : rows * t + 1, :] = down_above[rows - 1 : rows, :].astype(F32) + 1.0
        wtmp[rows * t + 1 : rows * (t + 1), :] = levels[0 : rows - 1, :]
    spread(3, (q_row > 0) | (pix > 0), 0)

    smooth = jnp.concatenate([smooth_in[...], smooth_in[...]], axis=1)
    lane = lax.broadcasted_iota(jnp.int32, (piece, 128), 1)

    def laplace(k):
        for copy in halos(k):
            copy.wait()
        if k == 0:
            window = ubuf[k, pl.ds(pl.multiple_of(piece * strip, 8), piece + 16), :]
        else:
            window = jnp.concatenate(
                [halo_recv[k, 2, 0:8, :], ubuf[k, my_rows(), :], halo_recv[k, 3, 0:8, :]], axis=0
            )
        mine = window[8 : 8 + piece]
        swapped = pltpu.roll(mine, 64, 1)
        before = pltpu.roll(window[8 - rows : 8 - rows + piece], 64, 1)
        after = pltpu.roll(window[8 + rows : 8 + rows + piece], 64, 1)
        right = jnp.where(lane < 64, swapped, after)
        left = jnp.where(lane < 64, before, swapped)
        shift[0] = window[7 : 7 + piece]
        shift[1] = window[9 : 9 + piece]
        shift[0, pl.ds(0, pairs, stride=rows), :] = halo_recv[k, 0, 0:pairs, :]
        shift[1, pl.ds(rows - 1, pairs, stride=rows), :] = halo_recv[k, 1, 0:pairs, :]
        flow = weights[0] * (mine - right) + weights[1] * (mine - left)
        flow = flow + weights[2] * (mine - shift[1]) + weights[3] * (mine - shift[0])
        return mine, flow * smooth

    for k in range(ITERS):
        mine, lap = laplace(k)
        drain(h_recv.at[k, pl.ds(0, group - 1)], h_rsem.at[k])
        h_recv[k, spot] = h_send[k, spot]
        total = h_recv[k, 0]
        for j in range(1, group):
            total = total + h_recv[k, j]
        z_recv[k, zed] = total
        each(n_z - 1, lambda i: send_z(k, i).start())
        if k == 0:
            x_copies[0].start()
        if k == ITERS - 1:
            c_copies[1].start()
        drain(g_recv.at[k, pl.ds(0, g_count(k) - 1)], g_rsem.at[k])
        if k == 0:
            g_recv[k, mz] = g_send[k, strip]
        else:
            g_recv[k, y] = g_send[k, y]
        total = g_recv[k, 0]
        for j in range(1, g_count(k)):
            total = total + g_recv[k, j]
        vsq = jnp.sum(total[piece:, :])
        eta_u = 1.0 / (jnp.full((1, 128), vsq, F32) / rank + 8.0 * smooth + 1.0)
        mine = mine - eta_u * (total[0:piece, :] + lap)
        ubuf[k + 1, my_rows(), :] = mine
        if k + 1 < ITERS:
            each(n_y - 1, lambda i: send_u(k + 1, 2 * y_peer(i) + side).start())
            send_halos(k + 1, mine)
            if k == 0:
                x_copies[1].start()
        else:
            def both_sides(i):
                send_u(k + 1, 2 * y_peer(i) + 1 - side, cross_rsem).start()
                send_u(k + 1, 2 * y_peer(i) + side).start()

            each(n_y - 1, both_sides)
            send_u(k + 1, 2 * y + 1 - side, cross_rsem).start()
        drain(z_recv.at[k, pl.ds(0, n_z - 1)], z_rsem.at[k])
        total = z_recv[k, 0]
        for j in range(1, n_z):
            total = total + z_recv[k, j]
        usq = jnp.sum(total[2 * srows :, :])
        eta_v = 1.0 / (jnp.full((1, 128), usq, F32) / rank + 1.0)
        if k == 0:
            v_copy.wait()
        for b in range(2):
            vbuf[k + 1, b, v_rows(), :] = (
                vbuf[k, b, v_rows(), :] - eta_v * total[b * srows : (b + 1) * srows, :]
            )
        each(group - 1, lambda i: send_v(k + 1, i).start())
        if k == 0:
            thr_copy.wait()
            for copy in x_copies:
                copy.wait()
        drain(ubuf.at[0, pl.ds(0, 2 * srows * (group - 1))], v_rsem.at[k])
        drain(ubuf.at[k + 1, pl.ds(8, piece * (n_y - 1))], u_rsem.at[k])
        if k + 1 < ITERS:
            usq = sweep(k + 1)
            h_part(k + 1, usq)
            start_g(k + 1)
            if k + 2 == ITERS:
                c_copies[0].start()

    def columns(which):
        return pl.ds(pl.multiple_of(which * (cols // 2), 128), cols // 2)

    def finish(which):
        width = cols // 2
        for r in range(rows):
            for par in range(2):
                xf[pl.ds(r * width + par, width // 2, stride=2), :] = x_other[
                    par, pl.ds(r, width // 2, stride=rows), :
                ]
        for r in range(rows):
            x_in[r, columns(which), :] = xf[r * width : (r + 1) * width, :].astype(BF16)
        return out_half(which)

    def out_half(which):
        return pltpu.make_async_copy(
            x_in.at[:, columns(which), :], so_ref.at[:, columns(which), :],
            out_sems.at[2 + (which + side) % 2],
        )

    sweep(ITERS, side)
    v_in[...] = vbuf[ITERS, side]
    outs = [
        pltpu.make_async_copy(src, dst, out_sems.at[i])
        for i, (src, dst) in enumerate([(u_in, uo_ref), (v_in, vo_ref)])
    ]
    outs[1].start()
    finish(side).start()
    drain(ubuf.at[ITERS, pl.ds(8, piece * n_y)], cross_rsem)
    for copy in c_copies:
        copy.wait()
    for t in range(cols // 2):
        u_in[:, 128 * t : 128 * (t + 1)] = ubuf[ITERS, 8 + rows * t : 8 + rows * (t + 1), :]
    outs[0].start()
    sweep(ITERS, 1 - side)
    finish(1 - side).start()

    for k in range(ITERS):
        drain(g_send.at[k, pl.ds(0, g_count(k) - 1)], g_ssem.at[k])
        drain(h_send.at[k, pl.ds(0, group - 1)], h_ssem.at[k])
        drain(z_recv.at[k, pl.ds(0, n_z - 1)], z_ssem.at[k])
        drain(ubuf.at[0, pl.ds(0, 2 * srows * (group - 1))], v_ssem.at[k])
        drain(ubuf.at[k + 1, pl.ds(8, piece * (u_count(k + 1) - 1))], u_ssem.at[k])
    for out in outs + [out_half(side), out_half(1 - side)]:
        out.wait()


def store(u_ref, v_ref, s_ref, uo_ref, vo_ref, so_ref, s, u, v, in_sems, out_sems):
    order = [(s_ref, s, so_ref), (u_ref, u, uo_ref), (v_ref, v, vo_ref)]
    loads = [pltpu.make_async_copy(a, b, in_sems.at[i]) for i, (a, b, _) in enumerate(order)]
    stores = [pltpu.make_async_copy(b, c, out_sems.at[i]) for i, (_, b, c) in enumerate(order)]
    for load in loads:
        load.start()
    for load, out in zip(loads, stores):
        load.wait()
        out.start()
    for out in stores:
        out.wait()


def shards(group, spectra, scores, loadings, smooth, thresholds, across, down):
    rows, cols, bins = spectra.shape
    rank = loadings.shape[1]
    n_pix, n_mz = lax.axis_size("pix"), lax.axis_size("mz")
    nq = rows * cols // 2
    half = nq // 2
    piece = nq // n_mz
    edge = max(piece // rows, 8)
    srows = rank // group
    n_z = 2 * (n_pix // group)
    hbm = pl.BlockSpec(memory_space=pltpu.HBM)
    anywhere = pl.BlockSpec(memory_space=pl.ANY)
    dma = pltpu.SemaphoreType.DMA
    vmem = pltpu.VMEM
    args = (
        spectra, scores, loadings.T, smooth.reshape(1, rank), thresholds.reshape(1, bins),
        across, down,
    )
    out_shape = (
        jax.ShapeDtypeStruct(scores.shape, F32),
        jax.ShapeDtypeStruct((rank, bins), F32),
        jax.ShapeDtypeStruct(spectra.shape, BF16),
    )
    outs = pl.pallas_call(
        functools.partial(kernel, group),
        out_shape=out_shape,
        in_specs=[hbm] * 7,
        out_specs=(anywhere,) * 3,
        scratch_shapes=[
            vmem(spectra.shape, BF16),
            vmem(scores.shape, F32),
            vmem((rank, bins), F32),
            vmem((1, rank), F32),
            vmem((1, bins), F32),
            vmem(across.shape, jnp.int32),
            vmem(down.shape, jnp.int32),
            vmem(down.shape, jnp.int32),
            vmem((rows * cols, bins), F32),
            vmem((2, nq, bins), F32),
            vmem((2, half, bins), F32),
            vmem((2, nq, bins), F32),
            vmem((2, half, bins), F32),
            vmem((nq, 256), BF16),
            vmem((nq, 2 * bins), BF16),
            vmem((nq, 2 * bins), BF16),
            vmem((2, 256, 2 * bins), BF16),
            vmem((2, 256, 2 * bins), BF16),
            vmem((ITERS + 1, nq + 16, 128), F32),
            vmem((ITERS + 1, 2, rank, bins), F32),
            vmem((1, bins), F32),
            vmem((ITERS, n_mz, piece + 1, 128), F32),
            vmem((ITERS, n_mz, piece + 1, 128), F32),
            vmem((ITERS, group, 2 * srows + 1, 128), F32),
            vmem((ITERS, group, 2 * srows + 1, 128), F32),
            vmem((ITERS, n_z, 2 * srows + 1, 128), F32),
            vmem((ITERS, 4, edge, 128), F32),
            vmem((ITERS, 4, edge, 128), F32),
            vmem((piece, cols), F32),
            vmem((2, piece, 128), F32),
            vmem((4, piece, 128), F32),
            dma((7,)),
            dma((4,)),
        ]
        + [dma((ITERS,))] * 10
        + [dma((ITERS, 4))] * 2
        + [dma] * 4
        + [dma((2,))] * 4
        + [dma] * 3,
        compiler_params=pltpu.CompilerParams(
            collective_id=0, has_side_effects=True, vmem_limit_bytes=63 * 1024 * 1024
        ),
        cost_estimate=pl.CostEstimate(
            flops=2 * 10 * rows * cols * bins * rank * 3,
            bytes_accessed=2 * (spectra.size * 2 + scores.size * 4),
            transcendentals=0,
        ),
    )(*args)
    score_maps, final, sparse = pl.pallas_call(
        store,
        out_shape=out_shape,
        in_specs=[hbm] * 3,
        out_specs=(hbm,) * 3,
        scratch_shapes=[
            vmem(spectra.shape, BF16),
            vmem(scores.shape, F32),
            vmem((rank, bins), F32),
            dma((3,)),
            dma((3,)),
        ],
        compiler_params=pltpu.CompilerParams(vmem_limit_bytes=63 * 1024 * 1024),
    )(*outs)
    return score_maps, final.T, sparse


def solution(mesh, group=GROUP):
    in_specs = (
        P("pix", None, "mz"),
        P("pix", None),
        P("mz", None),
        P(),
        P("mz"),
        P("pix", None),
        P("pix", None),
    )
    out_specs = (P("pix", None), P("mz", None), P("pix", None, "mz"))
    return jax.shard_map(
        functools.partial(shards, group), mesh=mesh, in_specs=in_specs, out_specs=out_specs,
        check_vma=False,
    )
```

```python
import functools
import jax
import jax.numpy as jnp
from jax import lax
from jax.experimental import pallas as pl
from jax.experimental.pallas import tpu as pltpu
from jax.sharding import PartitionSpec as P

ITERS = 3
GROUP = 8
MESH = pl.DeviceIdType.MESH
F32 = jnp.float32
BF16 = jnp.bfloat16
NT = (((1,), (1,)), ((), ()))
TN = (((0,), (0,)), ((), ()))


def mm(a, b, dims=(((1,), (0,)), ((), ()))):
    return lax.dot_general(a, b, dims, preferred_element_type=F32)


def split(a):
    high = a.astype(BF16)
    return high, (a - high.astype(F32)).astype(BF16)


def kernel(
    group,
    x_hbm, u_hbm, v_hbm, smooth_hbm, thr_hbm, across_hbm, down_hbm,
    uo_ref, vo_ref, so_ref,
    x_in, u_in, v_in, smooth_in, thr_in, across_in, down_in, down_above,
    xf, x_own, x_other, c_own, c_other, u_hl, d_h, d_l, b_hh, b_hl, ubuf, vbuf, thr_other,
    g_send, g_recv, h_send, h_recv, z_recv, halo_send, halo_recv,
    wtmp, shift, weights,
    in_sems, out_sems, g_ssem, g_rsem, u_ssem, u_rsem, h_ssem, h_rsem, z_ssem, z_rsem,
    v_ssem, v_rsem, halo_ssem, halo_rsem, down_ssem, down_rsem, thr_ssem, thr_rsem,
    x_ssem, x_rsem, c_ssem, c_rsem, cross_rsem, first_ssem, first_rsem,
):
    n_pix, n_mz = lax.axis_size("pix"), lax.axis_size("mz")
    pix, mz = lax.axis_index("pix"), lax.axis_index("mz")
    n_z, n_y = 2 * (n_pix // group), n_mz // 2
    block, spot = pix // group, pix % group
    y, side = mz // 2, mz % 2
    strip, zed = side * n_y + y, 2 * block + side
    twin = (pix, 2 * y + 1 - side)
    rows, cols, bins = x_in.shape
    rank = v_in.shape[0]
    nq = rows * cols // 2
    half = nq // 2
    piece = nq // n_mz
    pairs = piece // rows
    srows = rank // group
    below, above = (pix + 1) % n_pix, (pix + n_pix - 1) % n_pix

    barrier = pltpu.get_barrier_semaphore()

    def greet(device):
        pl.semaphore_signal(barrier, inc=1, device_id=device, device_id_type=MESH)

    def each(count, act):
        lax.fori_loop(0, count, lambda i, _: (act(i), 0)[1], 0)

    def far_first(at, i, n):
        return (at + n // 2 + ((i + 1) // 2) * (1 - 2 * (i % 2)) + n) % n

    def y_peer(i):
        return far_first(y, i, n_y)

    def mz_peer(i):
        return 2 * y_peer(i // 2) + (side + 1 - i % 2) % 2

    def group_device(i):
        return (block * group + far_first(spot, i, group), mz)

    def z_device(i):
        to = far_first(zed, i, n_z)
        return (to // 2 * group + spot, 2 * y + to % 2)

    def strip_device(j):
        return (pix, 2 * (j % n_y) + j // n_y)

    loads = [
        pltpu.make_async_copy(src, dst, in_sems.at[i])
        for i, (src, dst) in enumerate(
            [
                (u_hbm, u_in), (v_hbm, v_in), (x_hbm, x_in), (thr_hbm, thr_in),
                (down_hbm, down_in), (across_hbm, across_in), (smooth_hbm, smooth_in),
            ]
        )
    ]
    for load in loads:
        load.start()

    each(n_mz - 1, lambda i: greet((pix, mz_peer(i))))
    each(group - 1, lambda i: greet(group_device(i)))
    each(n_z - 1, lambda i: greet(z_device(i)))
    greet((below, mz))
    greet((above, mz))

    def remote(src, dst, ssem, rsem, device):
        return pltpu.make_async_remote_copy(
            src_ref=src, dst_ref=dst, send_sem=ssem, recv_sem=rsem,
            device_id=device, device_id_type=MESH,
        )

    def drain(ref, sem):
        pltpu.make_async_copy(ref, ref, sem).wait()

    def my_rows():
        return pl.ds(pl.multiple_of(8 + piece * strip, 8), piece)

    def half_rows(which, at=0, count=half):
        return pl.ds(pl.multiple_of(half * which + at, 8), count)

    zeros8 = jnp.zeros((8, 128), F32)
    ubuf[0, 0:8, :] = zeros8
    ubuf[0, 8 + nq : 16 + nq, :] = zeros8
    b_hh[...] = jnp.zeros_like(b_hh)
    b_hl[...] = jnp.zeros_like(b_hl)
    for load in loads[:4]:
        load.wait()
    for t in range(cols // 2):
        ubuf[0, 8 + rows * t : 8 + rows * (t + 1), :] = u_in[:, 128 * t : 128 * (t + 1)]
    vbuf[0, side] = v_in[...]
    xf[...] = x_in[...].reshape(rows * cols, bins).astype(F32)
    for r in range(rows):
        for par in range(2):
            x_own[par, pl.ds(r, cols // 2, stride=rows), :] = xf[
                pl.ds(r * cols + par, cols // 2, stride=2), :
            ]

    def halos(k):
        to = ((above, mz), (below, mz), strip_device((strip + n_mz - 1) % n_mz),
              strip_device((strip + 1) % n_mz))
        return [
            remote(
                halo_send.at[k, i], halo_recv.at[k, i ^ 1], halo_ssem.at[k, i],
                halo_rsem.at[k, i ^ 1], to[i],
            )
            for i in range(2 if k == 0 else 4)
        ]

    def send_halos(k, mine):
        shift[0] = mine
        halo_send[k, 0, 0:pairs, :] = shift[0, pl.ds(0, pairs, stride=rows), :]
        halo_send[k, 1, 0:pairs, :] = shift[0, pl.ds(rows - 1, pairs, stride=rows), :]
        halo_send[k, 2, 0:8, :] = mine[0:8]
        halo_send[k, 3, 0:8, :] = mine[piece - 8 : piece]
        for copy in halos(k):
            copy.start()

    chunk = 128

    def factors(k, slot):
        high, low = split(vbuf[k, side if slot == 0 else 1 - side])
        for at, part in ((0, high), (128, high)):
            b_hh[slot, at : at + rank, 0:bins] = part
            b_hh[slot, at + rank : at + 2 * rank, bins : 2 * bins] = part
        for at, part in ((0, high), (128, low)):
            b_hl[slot, at : at + rank, 0:bins] = part
            b_hl[slot, at + rank : at + 2 * rank, bins : 2 * bins] = part

    def sweep(k, which=None):
        paired = 0 < k < ITERS
        slots = (0, 1) if paired else (0,)
        for slot in slots if which is None or which is side else ():
            factors(k, slot)
        usq = zeros8
        for q in range(0, nq if k == 0 else half, chunk):
            here = pl.ds(q, chunk)
            own = here if k == 0 else half_rows(side if which is None else which, q, chunk)
            u = ubuf[k, pl.ds(pl.multiple_of(own.start + 8, 8), chunk), :]
            u_h, u_l = split(u)
            u_hl[here, 0:128] = u_h
            u_hl[here, 128:256] = u_l
            usq = usq + jnp.sum((u * u).reshape(chunk // 8, 8, 128), axis=0)
            for slot in slots:
                approx = mm(u_hl[here, :], b_hh[slot]) + mm(u_h, b_hl[slot, 128:256, :])
                thr = (thr_other if slot else thr_in)[...]
                x, c = (x_other, c_other) if slot else (x_own, c_own)
                spot_rows = here if slot else own
                dest = pl.ds(slot * half + q, chunk)
                for par in range(2):
                    lanes = slice(par * bins, (par + 1) * bins)
                    low = approx[:, lanes]
                    data = x[par, spot_rows, :]
                    if k == 0:
                        d = low - data
                    else:
                        t = data - low
                        if k > 1:
                            old = c[par, spot_rows, :]
                            t = t + old
                        clipped = jnp.clip(t, -thr, thr)
                        if k == ITERS:
                            x_other[par, here, :] = t - clipped
                            continue
                        c[par, spot_rows, :] = clipped
                        d = -2.0 * clipped
                        if k > 1:
                            d = d + old
                    high, low = split(d)
                    d_h[dest, lanes] = high
                    d_l[dest, lanes] = low
        return usq

    def products(k):
        slots = (0,) if k == 0 else (0, 1)
        vsq = jnp.zeros((1, 128), F32)
        for slot in slots:
            v = vbuf[k, side if slot == 0 else 1 - side]
            vsq = vsq + jnp.sum(v * v, axis=0, keepdims=True)
        for q in range(0, nq if k == 0 else half, chunk):
            g = None
            for slot in slots:
                dest = pl.ds(slot * half + q, chunk)
                g2 = mm(d_h[dest, :], b_hl[slot], NT)
                part = g2[:, 0:128] + g2[:, 128:256] + mm(d_l[dest, :], b_hh[slot, 0:128, :], NT)
                g = part if g is None else g + part
            for j in range(q // piece, (q + chunk) // piece):
                g_send[k, j, 0:piece, :] = g[j * piece - q : (j + 1) * piece - q, :]
                g_send[k, j, piece : piece + 1, :] = vsq

    def send_g(k, i):
        if k == 0:
            to = mz_peer(i)
            return remote(
                g_send.at[k, (to % 2) * n_y + to // 2], g_recv.at[k, mz], g_ssem.at[k],
                g_rsem.at[k], (pix, to),
            )
        to = y_peer(i)
        return remote(
            g_send.at[k, to], g_recv.at[k, y], g_ssem.at[k], g_rsem.at[k], (pix, 2 * to + side)
        )

    def send_h(k, i):
        return remote(
            h_send.at[k, far_first(spot, i, group)], h_recv.at[k, spot], h_ssem.at[k],
            h_rsem.at[k], group_device(i),
        )

    def send_z(k, i):
        ref = z_recv.at[k, zed]
        return remote(ref, ref, z_ssem.at[k], z_rsem.at[k], z_device(i))

    def v_rows():
        return pl.ds(pl.multiple_of(srows * spot, 8), srows)

    def send_v(k, i):
        ref = vbuf.at[k, pl.ds(0, 2), v_rows()]
        return remote(ref, ref, v_ssem.at[k - 1], v_rsem.at[k - 1], group_device(i))

    def send_u(k, to, rsem=None):
        ref = ubuf.at[k, my_rows()]
        rsem = u_rsem.at[k - 1] if rsem is None else rsem
        return remote(ref, ref, u_ssem.at[k - 1], rsem, (pix, to))

    def g_count(k):
        return n_mz if k == 0 else n_y

    def u_count(k):
        return n_mz if k == ITERS else n_y

    def start_g(k):
        each(g_count(k) - 1, lambda i: send_g(k, i).start())

    def h_part(k, usq):
        for slot in (0,) if k == 0 else (0, 1):
            n = nq if k == 0 else half
            dest = slice(slot * half, slot * half + n)
            both = mm(u_hl[0:n, :], d_h[dest, :], TN)
            prod = both[0:128, :] + both[128:256, :] + mm(u_hl[0:n, 0:128], d_l[dest, :], TN)
            h = prod[0:rank, 0:bins] + prod[rank : 2 * rank, bins : 2 * bins]
            at = srows * (side if slot == 0 else 1 - side)
            for j in range(group):
                h_send[k, j, pl.ds(pl.multiple_of(at, 8), srows), :] = h[
                    j * srows : (j + 1) * srows, :
                ]
        usq = jnp.sum(usq, axis=0, keepdims=True)
        if k == 0:
            usq = 0.5 * usq
            at = pl.ds(pl.multiple_of(srows * (1 - side), 8), srows)
            for j in range(group):
                h_send[k, j, at, :] = jnp.zeros((srows, 128), F32)
        for j in range(group):
            h_send[k, j, 2 * srows : 2 * srows + 1, :] = usq
        each(group - 1, lambda i: send_h(k, i).start())

    usq = sweep(0)
    products(0)
    pl.semaphore_wait(barrier, n_mz - 1 + group - 1 + n_z - 1 + 2)
    x_copies = [
        remote(
            x_own.at[par, half_rows(1 - side)], x_other.at[par], x_ssem.at[par], x_rsem.at[par],
            twin,
        )
        for par in range(2)
    ]
    start_g(0)
    h_part(0, usq)
    send_halos(0, ubuf[0, my_rows(), :])
    thr_copy = remote(thr_in, thr_other, thr_ssem, thr_rsem, twin)
    thr_copy.start()
    v_ref = vbuf.at[0, side]
    v_copy = remote(v_ref, v_ref, first_ssem, first_rsem, twin)
    v_copy.start()
    loads[4].wait()
    down_copy = remote(down_in, down_above, down_ssem, down_rsem, (below, mz))
    down_copy.start()
    c_copies = [
        remote(
            c_other.at[par], c_own.at[par, half_rows(side)], c_ssem.at[par], c_rsem.at[par],
            twin,
        )
        for par in range(2)
    ]

    for load in loads[5:]:
        load.wait()
    q_col = lax.broadcasted_iota(jnp.int32, (piece, cols), 0) // rows + pairs * strip
    q_row = lax.broadcasted_iota(jnp.int32, (piece, cols), 0) % rows
    col = lax.broadcasted_iota(jnp.int32, (piece, cols), 1)
    p_col = lax.broadcasted_iota(jnp.int32, (cols, 128), 0)
    p_half = lax.broadcasted_iota(jnp.int32, (cols, 128), 1) // 64

    def spread(which, keep, offset):
        pick = jnp.where(keep & ((col + offset) // 2 == q_col), wtmp[...], 0.0)
        place = jnp.where((p_col + offset) % 2 == p_half, 0.25, 0.0)
        weights[which] = mm(pick.astype(BF16), place.astype(BF16))

    levels = across_in[...].astype(F32) + 1.0
    for t in range(pairs):
        wtmp[rows * t : rows * (t + 1), :] = levels
    spread(0, col < cols - 1, 0)
    spread(1, col < cols - 1, 1)
    levels = down_in[...].astype(F32) + 1.0
    for t in range(pairs):
        wtmp[rows * t : rows * (t + 1), :] = levels
    spread(2, (q_row < rows - 1) | (pix < n_pix - 1), 0)
    down_copy.wait()
    for t in range(pairs):
        wtmp[rows * t : rows * t + 1, :] = down_above[rows - 1 : rows, :].astype(F32) + 1.0
        wtmp[rows * t + 1 : rows * (t + 1), :] = levels[0 : rows - 1, :]
    spread(3, (q_row > 0) | (pix > 0), 0)

    smooth = jnp.concatenate([smooth_in[...], smooth_in[...]], axis=1)
    lane = lax.broadcasted_iota(jnp.int32, (piece, 128), 1)

    def laplace(k):
        for copy in halos(k):
            copy.wait()
        if k == 0:
            window = ubuf[k, pl.ds(pl.multiple_of(piece * strip, 8), piece + 16), :]
        else:
            window = jnp.concatenate(
                [halo_recv[k, 2, 0:8, :], ubuf[k, my_rows(), :], halo_recv[k, 3, 0:8, :]], axis=0
            )
        mine = window[8 : 8 + piece]
        swapped = pltpu.roll(mine, 64, 1)
        before = pltpu.roll(window[8 - rows : 8 - rows + piece], 64, 1)
        after = pltpu.roll(window[8 + rows : 8 + rows + piece], 64, 1)
        right = jnp.where(lane < 64, swapped, after)
        left = jnp.where(lane < 64, before, swapped)
        shift[0] = window[7 : 7 + piece]
        shift[1] = window[9 : 9 + piece]
        shift[0, pl.ds(0, pairs, stride=rows), :] = halo_recv[k, 0, 0:pairs, :]
        shift[1, pl.ds(rows - 1, pairs, stride=rows), :] = halo_recv[k, 1, 0:pairs, :]
        flow = weights[0] * (mine - right) + weights[1] * (mine - left)
        flow = flow + weights[2] * (mine - shift[1]) + weights[3] * (mine - shift[0])
        return mine, flow * smooth

    for k in range(ITERS):
        mine, lap = laplace(k)
        drain(h_recv.at[k, pl.ds(0, group - 1)], h_rsem.at[k])
        h_recv[k, spot] = h_send[k, spot]
        total = h_recv[k, 0]
        for j in range(1, group):
            total = total + h_recv[k, j]
        z_recv[k, zed] = total
        each(n_z - 1, lambda i: send_z(k, i).start())
        if k == 0:
            x_copies[0].start()
        if k == ITERS - 1:
            c_copies[1].start()
        drain(g_recv.at[k, pl.ds(0, g_count(k) - 1)], g_rsem.at[k])
        if k == 0:
            g_recv[k, mz] = g_send[k, strip]
        else:
            g_recv[k, y] = g_send[k, y]
        total = g_recv[k, 0]
        for j in range(1, g_count(k)):
            total = total + g_recv[k, j]
        vsq = jnp.sum(total[piece:, :])
        eta_u = 1.0 / (jnp.full((1, 128), vsq, F32) / rank + 8.0 * smooth + 1.0)
        mine = mine - eta_u * (total[0:piece, :] + lap)
        ubuf[k + 1, my_rows(), :] = mine
        if k + 1 < ITERS:
            each(n_y - 1, lambda i: send_u(k + 1, 2 * y_peer(i) + side).start())
            send_halos(k + 1, mine)
            if k == 0:
                x_copies[1].start()
        else:
            def both_sides(i):
                send_u(k + 1, 2 * y_peer(i) + 1 - side, cross_rsem).start()
                send_u(k + 1, 2 * y_peer(i) + side).start()

            each(n_y - 1, both_sides)
            send_u(k + 1, 2 * y + 1 - side, cross_rsem).start()
        drain(z_recv.at[k, pl.ds(0, n_z - 1)], z_rsem.at[k])
        total = z_recv[k, 0]
        for j in range(1, n_z):
            total = total + z_recv[k, j]
        usq = jnp.sum(total[2 * srows :, :])
        eta_v = 1.0 / (jnp.full((1, 128), usq, F32) / rank + 1.0)
        if k == 0:
            v_copy.wait()
        for b in range(2):
            vbuf[k + 1, b, v_rows(), :] = (
                vbuf[k, b, v_rows(), :] - eta_v * total[b * srows : (b + 1) * srows, :]
            )
        each(group - 1, lambda i: send_v(k + 1, i).start())
        if k == 0:
            thr_copy.wait()
            for copy in x_copies:
                copy.wait()
        drain(ubuf.at[0, pl.ds(0, 2 * srows * (group - 1))], v_rsem.at[k])
        drain(ubuf.at[k + 1, pl.ds(8, piece * (n_y - 1))], u_rsem.at[k])
        if k + 1 < ITERS:
            usq = sweep(k + 1)
            h_part(k + 1, usq)
            products(k + 1)
            start_g(k + 1)
            if k + 2 == ITERS:
                c_copies[0].start()

    def columns(which):
        return pl.ds(pl.multiple_of(which * (cols // 2), 128), cols // 2)

    def finish(which):
        width = cols // 2
        for r in range(rows):
            for par in range(2):
                xf[pl.ds(r * width + par, width // 2, stride=2), :] = x_other[
                    par, pl.ds(r, width // 2, stride=rows), :
                ]
        for r in range(rows):
            x_in[r, columns(which), :] = xf[r * width : (r + 1) * width, :].astype(BF16)
        return out_half(which)

    def out_half(which):
        return pltpu.make_async_copy(
            x_in.at[:, columns(which), :], so_ref.at[:, columns(which), :],
            out_sems.at[2 + (which + side) % 2],
        )

    sweep(ITERS, side)
    v_in[...] = vbuf[ITERS, side]
    outs = [
        pltpu.make_async_copy(src, dst, out_sems.at[i])
        for i, (src, dst) in enumerate([(u_in, uo_ref), (v_in, vo_ref)])
    ]
    outs[1].start()
    finish(side).start()
    drain(ubuf.at[ITERS, pl.ds(8, piece * n_y)], cross_rsem)
    for copy in c_copies:
        copy.wait()
    for t in range(cols // 2):
        u_in[:, 128 * t : 128 * (t + 1)] = ubuf[ITERS, 8 + rows * t : 8 + rows * (t + 1), :]
    outs[0].start()
    sweep(ITERS, 1 - side)
    finish(1 - side).start()

    for k in range(ITERS):
        drain(g_send.at[k, pl.ds(0, g_count(k) - 1)], g_ssem.at[k])
        drain(h_send.at[k, pl.ds(0, group - 1)], h_ssem.at[k])
        drain(z_recv.at[k, pl.ds(0, n_z - 1)], z_ssem.at[k])
        drain(ubuf.at[0, pl.ds(0, 2 * srows * (group - 1))], v_ssem.at[k])
        drain(ubuf.at[k + 1, pl.ds(8, piece * (u_count(k + 1) - 1))], u_ssem.at[k])
    for out in outs + [out_half(side), out_half(1 - side)]:
        out.wait()


def store(u_ref, v_ref, s_ref, uo_ref, vo_ref, so_ref, s, u, v, in_sems, out_sems):
    order = [(s_ref, s, so_ref), (u_ref, u, uo_ref), (v_ref, v, vo_ref)]
    loads = [pltpu.make_async_copy(a, b, in_sems.at[i]) for i, (a, b, _) in enumerate(order)]
    stores = [pltpu.make_async_copy(b, c, out_sems.at[i]) for i, (_, b, c) in enumerate(order)]
    for load in loads:
        load.start()
    for load, out in zip(loads, stores):
        load.wait()
        out.start()
    for out in stores:
        out.wait()


def shards(group, spectra, scores, loadings, smooth, thresholds, across, down):
    rows, cols, bins = spectra.shape
    rank = loadings.shape[1]
    n_pix, n_mz = lax.axis_size("pix"), lax.axis_size("mz")
    nq = rows * cols // 2
    half = nq // 2
    piece = nq // n_mz
    edge = max(piece // rows, 8)
    srows = rank // group
    n_z = 2 * (n_pix // group)
    hbm = pl.BlockSpec(memory_space=pltpu.HBM)
    anywhere = pl.BlockSpec(memory_space=pl.ANY)
    dma = pltpu.SemaphoreType.DMA
    vmem = pltpu.VMEM
    args = (
        spectra, scores, loadings.T, smooth.reshape(1, rank), thresholds.reshape(1, bins),
        across, down,
    )
    out_shape = (
        jax.ShapeDtypeStruct(scores.shape, F32),
        jax.ShapeDtypeStruct((rank, bins), F32),
        jax.ShapeDtypeStruct(spectra.shape, BF16),
    )
    outs = pl.pallas_call(
        functools.partial(kernel, group),
        out_shape=out_shape,
        in_specs=[hbm] * 7,
        out_specs=(anywhere,) * 3,
        scratch_shapes=[
            vmem(spectra.shape, BF16),
            vmem(scores.shape, F32),
            vmem((rank, bins), F32),
            vmem((1, rank), F32),
            vmem((1, bins), F32),
            vmem(across.shape, jnp.int32),
            vmem(down.shape, jnp.int32),
            vmem(down.shape, jnp.int32),
            vmem((rows * cols, bins), F32),
            vmem((2, nq, bins), F32),
            vmem((2, half, bins), F32),
            vmem((2, nq, bins), F32),
            vmem((2, half, bins), F32),
            vmem((nq, 256), BF16),
            vmem((nq, 2 * bins), BF16),
            vmem((nq, 2 * bins), BF16),
            vmem((2, 256, 2 * bins), BF16),
            vmem((2, 256, 2 * bins), BF16),
            vmem((ITERS + 1, nq + 16, 128), F32),
            vmem((ITERS + 1, 2, rank, bins), F32),
            vmem((1, bins), F32),
            vmem((ITERS, n_mz, piece + 1, 128), F32),
            vmem((ITERS, n_mz, piece + 1, 128), F32),
            vmem((ITERS, group, 2 * srows + 1, 128), F32),
            vmem((ITERS, group, 2 * srows + 1, 128), F32),
            vmem((ITERS, n_z, 2 * srows + 1, 128), F32),
            vmem((ITERS, 4, edge, 128), F32),
            vmem((ITERS, 4, edge, 128), F32),
            vmem((piece, cols), F32),
            vmem((2, piece, 128), F32),
            vmem((4, piece, 128), F32),
            dma((7,)),
            dma((4,)),
        ]
        + [dma((ITERS,))] * 10
        + [dma((ITERS, 4))] * 2
        + [dma] * 4
        + [dma((2,))] * 4
        + [dma] * 3,
        compiler_params=pltpu.CompilerParams(
            collective_id=0, has_side_effects=True, vmem_limit_bytes=63 * 1024 * 1024
        ),
        cost_estimate=pl.CostEstimate(
            flops=2 * 10 * rows * cols * bins * rank * 3,
            bytes_accessed=2 * (spectra.size * 2 + scores.size * 4),
            transcendentals=0,
        ),
    )(*args)
    score_maps, final, sparse = pl.pallas_call(
        store,
        out_shape=out_shape,
        in_specs=[hbm] * 3,
        out_specs=(hbm,) * 3,
        scratch_shapes=[
            vmem(spectra.shape, BF16),
            vmem(scores.shape, F32),
            vmem((rank, bins), F32),
            dma((3,)),
            dma((3,)),
        ],
        compiler_params=pltpu.CompilerParams(vmem_limit_bytes=63 * 1024 * 1024),
    )(*outs)
    return score_maps, final.T, sparse


def solution(mesh, group=GROUP):
    in_specs = (
        P("pix", None, "mz"),
        P("pix", None),
        P("mz", None),
        P(),
        P("mz"),
        P("pix", None),
        P("pix", None),
    )
    out_specs = (P("pix", None), P("mz", None), P("pix", None, "mz"))
    return jax.shard_map(
        functools.partial(shards, group), mesh=mesh, in_specs=in_specs, out_specs=out_specs,
        check_vma=False,
    )
```
